256 devices in a mesh: slab: 64 (over z, x, core), ang: 4 (over y).
Axes of the slice: x: 4, y: 4, z: 8, core: 2. Of those that a mesh axis runs over, the one named last changes fastest.
Arguments:
- projections: float32 [8, 64, 16, 4096], P('ang', 'slab'), may hold values from -6 to 6
- weights: bfloat16 [8, 32, 3, 128, 128], P('ang'), may hold values from -0.3125 to 0.3125
- columns: int32 [8, 32, 3], P('ang'), may hold values from 0 to 31, as said below
- row_weights: float32 [8, 64, 3, 1, 4], P('ang', 'slab'), may hold values from -3 to 3
- reach: int32 [8, 64, 2], P('ang', 'slab'), may hold values from -1 to 1, as said below
Outputs:
- volume: float32 [256, 16, 4096], P('slab')
- residual: float32 [8, 64, 16, 4096], P('ang', 'slab')
- gradient: float32 [256, 16, 4096], P('slab')
The draws below stay inside these ranges and needn't reach their ends.
Inputs may be any that keep to these rules, and one draw needn't show every extreme that they name: `columns`: each footprint names 3 consecutive blocks; the first detector column block starts at block 0 and the last ends at block 31 at every angle. `reach`: the first entry is -1 or 0 and the second 0 or 1; the first slab never reaches below, the last never above; at every angle slab 1 reaches the band below, slab 64 - 2 reaches the band above, and the two middle slabs reach both neighbours' bands; other slabs far from the centre reach their neighbours' bands more often.
All inputs are finite; a program needn't handle non-finite values.
Results may differ from the reference program's by a relative error of at most 0.0095.
Values may be sent and summed in bfloat16 or wider, within the bound.
No kernel may reach another device: no remote copies, remote signals or barrier semaphores. Data moves between devices by JAX's collectives and lax.ppermute only.
A program may use at most 128 MiB of HBM per device.

```python
import jax
import jax.numpy as jnp
from jax import lax

ZD = 4
VB = 1
L = 16
X = 4096
U = 4096
K = 3
ITERS = 2
SLABS = 64
Z = 256
V = 64
ANGLES = 8
UB = 32
XB = 32


def draw_columns(key, part):
    key = jax.random.fold_in(key, 11)
    jitter = jax.random.randint(key, (ANGLES, UB), -2, 3)
    blocks_at = jnp.arange(UB, dtype=jnp.int32)
    centre = blocks_at * XB // UB
    start = jnp.clip(centre[None, :] + jitter - K // 2, 0, XB - K)
    start = jnp.where((blocks_at == 0)[None, :], 0, start)
    start = jnp.where((blocks_at == UB - 1)[None, :], XB - K, start)
    return (start[..., None] + jnp.arange(K, dtype=jnp.int32)).astype(jnp.int32)


def draw_reach(key, part):
    key = jax.random.fold_in(key, 23)
    slab_at = jnp.arange(SLABS, dtype=jnp.int32)
    distance = jnp.abs(2 * slab_at - SLABS + 1)
    tosses = jax.random.randint(key, (ANGLES, SLABS, 2), 0, SLABS)
    middle = (slab_at == SLABS // 2) | (slab_at == SLABS // 2 - 1)
    lower_on = ((tosses[..., 0] < distance[None, :]) | (slab_at == 1)[None, :] | middle[None, :]) & (slab_at > 0)[None, :]
    upper_on = ((tosses[..., 1] < distance[None, :]) | (slab_at == SLABS - 2)[None, :] | middle[None, :]) & (slab_at < SLABS - 1)[None, :]
    lower_val = jnp.where(lower_on, -1, 0)
    upper_val = jnp.where(upper_on, 1, 0)
    return jnp.stack([lower_val, upper_val], axis=-1).astype(jnp.int32)


def levels(own_key, extent, cuts, low, top_value):
    def one(axis_at, parts):
        steps = jax.random.uniform(jax.random.fold_in(jax.random.fold_in(own_key, 6), axis_at), (parts,), jnp.float32, low / len(cuts), top_value / len(cuts))
        return jnp.repeat(jnp.exp(steps), extent[axis_at] // parts).reshape((-1,) + (1,) * (len(extent) - axis_at - 1))

    factor_of = one(*cuts[0])
    for cut in cuts[1:]:
        factor_of = factor_of * one(*cut)
    return factor_of


def gaussian(stream_key, shape, scale, bound, shards=(), held_as=jnp.bfloat16):
    factor_of = levels(stream_key, shape, shards, -0.22, 0.18) if shards else 1.0
    values = jax.random.normal(stream_key, shape, jnp.float32) * scale * factor_of
    return jnp.minimum(jnp.maximum(values, -bound), bound).astype(held_as)


def setup_inputs(seed: int = 0) -> dict:
    seeds = jax.random.split(jax.random.key(seed), 6)
    return {
        "projections": gaussian(seeds[0], (ANGLES, V, L, U), 1.0, 6.0, ((0, 4), (1, 64)), jnp.float32),
        "weights": gaussian(seeds[1], (ANGLES, UB, K, 128, 128), (K * 128) ** -0.5, 0.3125, ((0, 4),)),
        "columns": draw_columns(jax.random.fold_in(seeds[5], 71), 0),
        "row_weights": gaussian(seeds[3], (ANGLES, SLABS, 3, VB, ZD), 0.5, 3.0, ((0, 4), (1, 64)), jnp.float32),
        "reach": draw_reach(jax.random.fold_in(seeds[5], 71), 0),
    }


HIGH = lax.Precision.HIGHEST


def masked_rows(row_weights, reach):
    lower_on = (reach[..., 0] == -1).astype(jnp.float32)
    upper_on = (reach[..., 1] == 1).astype(jnp.float32)
    factor = jnp.stack([lower_on, jnp.ones_like(lower_on), upper_on], axis=-1)
    return row_weights * factor[..., None, None]


def footprint(slices_b, col_table, weight_table):
    blocks = slices_b.reshape(slices_b.shape[0], XB, 128).astype(jnp.float32)
    gathered = blocks[:, col_table, :]
    result = jnp.einsum("nbki,bkiu->nbu", gathered, weight_table.astype(jnp.float32), precision=HIGH)
    return result.reshape(slices_b.shape[0], U)


def spread_back(spread_b, col_table, weight_table):
    contrib = jnp.einsum("nbu,bkiu->nbki", spread_b.reshape(-1, UB, 128).astype(jnp.float32), weight_table.astype(jnp.float32), precision=HIGH)
    onehot = (col_table[..., None] == jnp.arange(XB, dtype=jnp.int32)).astype(jnp.float32)
    return jnp.einsum("nbki,bkc->nci", contrib, onehot, precision=HIGH).reshape(-1, X)


def forward_all(direction, columns, weights, rows):
    slices_b = direction.astype(jnp.bfloat16).reshape(Z * L, X)
    zero_band = jnp.zeros((1, VB, L, U), jnp.float32)
    results = []
    for angle in range(ANGLES):
        images = footprint(slices_b, columns[angle], weights[angle]).reshape(SLABS, ZD, L, U)
        pieces = jnp.einsum("sdvz,szlu->sdvlu", rows[angle], images, precision=HIGH)
        band_sum = pieces[:, 1] + jnp.concatenate([zero_band, pieces[:-1, 2]], 0) + jnp.concatenate([pieces[1:, 0], zero_band], 0)
        results.append(band_sum.reshape(V, L, U))
    return jnp.stack(results)


def backward_all(residual, columns, weights, rows):
    zero_band = jnp.zeros((1, VB, L, U), jnp.float32)
    totals = jnp.zeros((Z * L, X), jnp.float32)
    for angle in range(ANGLES):
        bands = residual[angle].reshape(SLABS, VB, L, U)
        near = jnp.stack([jnp.concatenate([zero_band, bands[:-1]], 0), bands, jnp.concatenate([bands[1:], zero_band], 0)], 1)
        spread = jnp.einsum("sdvz,sdvlu->szlu", rows[angle], near, precision=HIGH)
        spread_b = spread.astype(jnp.bfloat16).reshape(Z * L, U)
        totals = totals + spread_back(spread_b, columns[angle], weights[angle])
    return totals.reshape(Z, L, X)


def reference(projections, weights, columns, row_weights, reach):
    rows = masked_rows(row_weights, reach)
    residual = projections
    gradient = backward_all(residual, columns, weights, rows)
    gamma_now = jnp.sum(gradient * gradient)
    direction = gradient
    volume = jnp.zeros_like(gradient)
    for sweep in range(ITERS):
        image_dir = forward_all(direction, columns, weights, rows)
        step_size = gamma_now / jnp.sum(image_dir * image_dir)
        volume = volume + step_size * direction
        residual = residual - step_size * image_dir
        gradient = backward_all(residual, columns, weights, rows)
        if sweep + 1 < ITERS:
            gamma_next = jnp.sum(gradient * gradient)
            direction = gradient + (gamma_next / gamma_now) * direction
            gamma_now = gamma_next
    return volume, residual, gradient
```

```python
import functools

import jax
import jax.numpy as jnp
from jax import lax
from jax.experimental import pallas as pl
from jax.experimental.pallas import tpu as pltpu
from jax.sharding import PartitionSpec as P

F32 = jnp.float32
BF16 = jnp.bfloat16
ANG = 4
PAIR = 2
L = 16
X = 4096
Q = X // ANG
UB = 32
ZD = 4
CH = 256
GROUP = 8
VMEM = pl.BlockSpec(memory_space=pltpu.VMEM)
SMEM = pl.BlockSpec(memory_space=pltpu.SMEM)
ANY = pl.BlockSpec(memory_space=pl.ANY)
LIMIT = 40 * 1024 * 1024


def call(kernel, outs, specs, scratch=(), flops=0, nbytes=2_000_000):
    return pl.pallas_call(
        kernel,
        out_shape=outs,
        in_specs=specs,
        out_specs=[VMEM] * len(outs),
        scratch_shapes=list(scratch),
        compiler_params=pltpu.CompilerParams(vmem_limit_bytes=LIMIT),
        cost_estimate=pl.CostEstimate(flops=flops, bytes_accessed=nbytes, transcendentals=0),
    )


def sds(shape, dtype):
    return jax.ShapeDtypeStruct(shape, dtype)


def halves(value):
    high = value.astype(BF16)
    low = (value - high.astype(F32)).astype(BF16)
    return jnp.concatenate([high, low], axis=0)


def fold(value):
    total = value[:8] + value[8:]
    out = total[:, :128]
    for at in range(1, total.shape[1] // 128):
        out = out + total[:, 128 * at:128 * (at + 1)]
    return out


def weight_copies(w_hbm, w_buf, sem):
    return [
        pltpu.make_async_copy(
            w_hbm.at[a, pl.ds(GROUP * g, GROUP)], w_buf.at[a, pl.ds(GROUP * g, GROUP)],
            sem.at[a, g],
        )
        for a in range(PAIR)
        for g in range(UB // GROUP)
    ]


def window(cols, a, block):
    return pl.ds(pl.multiple_of(cols[a, block] * 128, 128), 384)


def back_block(a, block, value, cols, w_buf, acc):
    both = halves(value)
    spread = lax.dot_general(
        both, w_buf[a, block], (((1,), (1,)), ((), ())), preferred_element_type=F32
    )
    at = window(cols, a, block)
    acc[a, :, at] += spread[:L] + spread[L:]


def send_shares(me, acc, outs):
    for r in range(ANG):
        quarter = lax.rem(me + r, ANG)
        outs[r][...] = acc[:, :, pl.ds(pl.multiple_of(quarter * Q, Q), Q)].astype(BF16)


def back_kernel(me_ref, cols, p_ref, w_hbm, o0, o1, o2, o3, w_buf, acc, sem):
    copies = weight_copies(w_hbm, w_buf, sem)
    for copy in copies:
        copy.start()
    acc[...] = jnp.zeros_like(acc)
    for a in range(PAIR):
        for g in range(UB // GROUP):
            copies[a * (UB // GROUP) + g].wait()
            for i in range(GROUP):
                block = g * GROUP + i
                back_block(a, block, p_ref[a, :, 128 * block:128 * (block + 1)], cols, w_buf, acc)
    send_shares(me_ref[0], acc, (o0, o1, o2, o3))


def both_body(cols, w_hbm, w_buf, acc, sem, copies, lhs, store):
    acc[...] = jnp.zeros_like(acc)
    for a in range(PAIR):
        for g in range(UB // GROUP):
            copies[a * (UB // GROUP) + g].wait()
            images = []
            for i in range(GROUP):
                block = g * GROUP + i
                image = jnp.dot(lhs(a, window(cols, a, block)), w_buf[a, block], preferred_element_type=F32)
                if image.shape[0] > L:
                    image = image[:L] + image[L:]
                store(a, block, image)
                images.append(image)
            for i in range(GROUP):
                back_block(a, g * GROUP + i, images[i], cols, w_buf, acc)


def gather_shares(me, shares, dst):
    for r in range(ANG):
        quarter = lax.rem(me + ANG - r, ANG)
        dst[:, :, pl.ds(pl.multiple_of(quarter * Q, Q), Q)] = shares[r][...]


def first_kernel(me_ref, cols, h0, h1, h2, h3, gam_ref, w_hbm,
                 o0, o1, o2, o3, h_out, q_out, dots, w_buf, acc, sem):
    copies = weight_copies(w_hbm, w_buf, sem)
    for copy in copies:
        copy.start()
    gather_shares(me_ref[0], (h0, h1, h2, h3), h_out)

    def lhs(a, at):
        return h_out[a, :, at]

    def store(a, block, image):
        q_out[a, :, 128 * block:128 * (block + 1)] = image

    both_body(cols, w_hbm, w_buf, acc, sem, copies, lhs, store)
    total = jnp.zeros((8, 128), F32)
    for a in range(PAIR):
        total = total + fold(q_out[a] * q_out[a])
    dots[:8] = gam_ref[...]
    dots[8:] = total
    send_shares(me_ref[0], acc, (o0, o1, o2, o3))


def second_kernel(me_ref, cols, h0, h1, h2, h3, sums_ref, before_ref, q0_ref, g0_ref, z0_ref, w_hbm,
                  o0, o1, o2, o3, w_out, dots, hz, high, low, w_buf, acc, sem):
    copies = weight_copies(w_hbm, w_buf, sem)
    for copy in copies:
        copy.start()
    step = jnp.sum(sums_ref[:8]) / jnp.sum(sums_ref[8:16])
    gather_shares(me_ref[0], (h0, h1, h2, h3), hz)
    for a in range(PAIR):
        value = before_ref[a].astype(F32) - step * hz[a].astype(F32)
        top = value.astype(BF16)
        high[a] = top
        low[a] = (value - top.astype(F32)).astype(BF16)

    def lhs(a, at):
        return jnp.concatenate([high[a, :, at], low[a, :, at]], axis=0)

    def store(a, block, image):
        w_out[a, :, 128 * block:128 * (block + 1)] = image

    both_body(cols, w_hbm, w_buf, acc, sem, copies, lhs, store)
    send_shares(me_ref[0], acc, (o0, o1, o2, o3))
    norm = jnp.zeros((8, 128), F32)
    for z in range(ZD):
        gradient = g0_ref[z] - step * z0_ref[z]
        norm = norm + fold(gradient * gradient)
    own = jnp.zeros((8, 128), F32)
    cross = jnp.zeros((8, 128), F32)
    for a in range(PAIR):
        own = own + fold(w_out[a] * w_out[a])
        cross = cross + fold(w_out[a] * q0_ref[a])
    dots[:8] = norm
    dots[8:16] = own
    dots[16:] = cross


def combine_kernel(k0, k1, k2, k3, c0, c1, c2, c3, t1, up, down, up_far, down_far):
    coefs = (k0, k1, k2, k3)
    parts = (c0, c1, c2, c3)
    for at in range(Q // CH):
        cut = pl.ds(at * CH, CH)
        totals = [None] * 12
        for r in range(ANG):
            for i in range(PAIR):
                value = parts[r][i, :, cut].astype(F32)
                for e in range(12):
                    term = coefs[r][12 * i + e] * value
                    totals[e] = term if totals[e] is None else totals[e] + term
        for z in range(ZD):
            below, own, above = totals[z], totals[4 + z], totals[8 + z]
            t1[z, :, cut] = own
            up[z, :, cut] = own.astype(BF16)
            down[z, :, cut] = own.astype(BF16)
            up[4 + z, :, cut] = above.astype(BF16)
            down[4 + z, :, cut] = below.astype(BF16)
            up_far[z, :, cut] = above.astype(BF16)
            down_far[z, :, cut] = below.astype(BF16)


def pieces_kernel(k0, k1, k2, k3, t1, up, down, from_low, from_high, far_low, far_high,
                  g_out, h0, h1, h2, h3, dots):
    coefs = (k0, k1, k2, k3)
    outs = (h0, h1, h2, h3)
    norm = jnp.zeros((8, 128), F32)
    for at in range(Q // CH):
        cut = pl.ds(at * CH, CH)

        def get(ref, z):
            return ref[z, :, cut].astype(F32)

        cells = []
        for z in range(ZD):
            cells.append(get(from_low, z) + get(far_low, z) + get(down, 4 + z))
        for z in range(ZD):
            value = t1[z, :, cut] + get(from_low, 4 + z) + get(from_high, 4 + z)
            g_out[z, :, cut] = value
            norm = norm + fold(value * value)
            cells.append(value)
        for z in range(ZD):
            cells.append(get(from_high, z) + get(far_high, z) + get(up, 4 + z))
        for r in range(ANG):
            for i in range(PAIR):
                total = None
                for e in range(12):
                    term = coefs[(ANG - r) % ANG][12 * i + e] * cells[e]
                    total = term if total is None else total + term
                outs[r][i, :, cut] = total.astype(BF16)
    dots[...] = norm


def last_kernel(k0, k1, k2, k3, c0, c1, c2, c3, t1, up, down):
    coefs = (k0, k1, k2, k3)
    parts = (c0, c1, c2, c3)
    for at in range(Q // CH):
        cut = pl.ds(at * CH, CH)
        totals = [None] * 12
        for r in range(ANG):
            for i in range(PAIR):
                value = parts[r][i, :, cut].astype(F32)
                for e in range(12):
                    term = coefs[r][12 * i + e] * value
                    totals[e] = term if totals[e] is None else totals[e] + term
        for z in range(ZD):
            t1[z, :, cut] = totals[4 + z]
            down[z, :, cut] = totals[z].astype(BF16)
            up[z, :, cut] = totals[8 + z].astype(BF16)


def scalars(first, second):
    gamma0 = jnp.sum(first[:8])
    curve0 = jnp.sum(first[8:16])
    gamma1 = jnp.sum(second[:8])
    own = jnp.sum(second[8:16])
    cross = jnp.sum(second[16:24])
    step0 = gamma0 / curve0
    ratio = gamma1 / gamma0
    curve1 = own + 2.0 * ratio * cross + ratio * ratio * curve0
    return step0, ratio, gamma1 / curve1


def finish_kernel(first, second, t1, from_low, from_high, g0, z0, out):
    step0, ratio, step1 = scalars(first, second)
    for z in range(ZD):
        last = t1[z] + from_low[z].astype(F32) + from_high[z].astype(F32)
        gradient = g0[z] - step0 * z0[z]
        out[z] = (step0 * g0[z] + step1 * (gradient + ratio * g0[z])).astype(BF16)
        out[ZD + z] = (gradient - step1 * (last + ratio * z0[z])).astype(BF16)


def residual_kernel(first, second, p, q0, w1, out):
    step0, ratio, step1 = scalars(first, second)
    for a in range(PAIR):
        out[a] = p[a] - step0 * q0[a] - step1 * (w1[a] + ratio * q0[a])


def place_kernel(me_ref, s0, s1, s2, s3, volume, gradient):
    for r, share in enumerate((s0, s1, s2, s3)):
        quarter = lax.rem(me_ref[0] + ANG - r, ANG)
        at = pl.ds(pl.multiple_of(quarter * Q, Q), Q)
        volume[:, :, at] = share[:ZD].astype(F32)
        gradient[:, :, at] = share[ZD:].astype(F32)


def along_ang(value, steps):
    return lax.ppermute(value, "ang", [(i, (i + steps) % ANG) for i in range(ANG)])


def along_slab(value, steps):
    count = lax.axis_size("slab")
    pairs = [(i, i + steps) for i in range(count) if 0 <= i + steps < count]
    return lax.ppermute(value, "slab", pairs)


def exchange(shares):
    far = along_ang(shares[2], 2)
    near = along_ang(shares[1], 1)
    back = along_ang(shares[3], 3)
    return (shares[0], near, far, back)


def total_of(value):
    count = lax.axis_size("slab")

    def stage(value, axis, perms):
        moved = [lax.ppermute(value, axis, perm) for perm in perms]
        return (value + moved[0]) + (moved[1] + moved[2])

    value = stage(value, "ang", [[(i, i ^ b) for i in range(ANG)] for b in (1, 2, 3)])
    for bits in ((2, 4), (16, 32), (1, 8)):
        low, high = bits
        value = stage(value, "slab", [[(i, i ^ b) for i in range(count)] for b in (low, high, low + high)])
    return value


def per_device(projections, weights, columns, row_weights, reach):
    lower_on = (reach[..., 0] == -1).astype(F32)
    upper_on = (reach[..., 1] == 1).astype(F32)
    factor = jnp.stack([lower_on, jnp.ones_like(lower_on), upper_on], axis=-1)
    rows = (row_weights * factor[..., None, None])[:, 0, :, 0, :]
    stencil = jnp.stack(
        [along_slab(rows[:, 2], 1), rows[:, 1], along_slab(rows[:, 0], -1)], axis=1
    ).reshape(PAIR * 12)
    coefs = exchange((stencil,) * 4)

    me = lax.axis_index("ang").astype(jnp.int32).reshape(1)
    cols = columns[:, :, 0]
    w = weights.reshape(PAIR, UB, 384, 128)
    p = projections.reshape(PAIR, L, X)

    share = sds((PAIR, L, Q), BF16)
    full = sds((PAIR, L, X), F32)
    part = sds((ZD, L, Q), F32)
    part_b = sds((ZD, L, Q), BF16)
    two_b = sds((2 * ZD, L, Q), BF16)
    dot1 = sds((8, 128), F32)
    w_scratch = [
        pltpu.VMEM((PAIR, UB, 384, 128), BF16),
        pltpu.VMEM((PAIR, L, X), F32),
        pltpu.SemaphoreType.DMA((PAIR, UB // GROUP)),
    ]
    macs = 2 * PAIR * L * UB * 384 * 128

    def axial(shares):
        t1, up, down, up_far, down_far = call(
            combine_kernel, [part, two_b, two_b, part_b, part_b], [SMEM] * 4 + [VMEM] * 4, flops=10_000_000
        )(*coefs, *shares)
        from_low = along_slab(up, 1)
        from_high = along_slab(down, -1)
        far_low = along_slab(up_far, 2)
        far_high = along_slab(down_far, -2)
        gradient, h0, h1, h2, h3, norm = call(
            pieces_kernel, [part] + [share] * 4 + [dot1], [SMEM] * 4 + [VMEM] * 7, flops=10_000_000
        )(*coefs, t1, up, down, from_low, from_high, far_low, far_high)
        return gradient, exchange((h0, h1, h2, h3)), norm

    shares = call(
        back_kernel, [share] * 4, [SMEM, SMEM, VMEM, ANY], w_scratch, flops=2 * macs, nbytes=7_000_000
    )(me, cols, p, w)
    g0, h, gamma = axial(exchange(shares))

    *shares, before, q0, first = call(
        first_kernel, [share] * 4 + [sds((PAIR, L, X), BF16), full, sds((16, 128), F32)],
        [SMEM, SMEM] + [VMEM] * 5 + [ANY], w_scratch, flops=3 * macs, nbytes=7_000_000,
    )(me, cols, *h, gamma, w)
    first = total_of(first)
    z0, h, _ = axial(exchange(shares))

    *shares, w1, second = call(
        second_kernel, [share] * 4 + [full, sds((24, 128), F32)],
        [SMEM, SMEM] + [VMEM] * 9 + [ANY],
        [pltpu.VMEM((PAIR, L, X), BF16)] * 3 + w_scratch, flops=4 * macs, nbytes=9_000_000,
    )(me, cols, *h, first, before, q0, g0, z0, w)
    second = total_of(second)
    t1, up, down = call(
        last_kernel, [part, part_b, part_b], [SMEM] * 4 + [VMEM] * 4, flops=10_000_000
    )(*coefs, *exchange(shares))
    from_low = along_slab(up, 1)
    from_high = along_slab(down, -1)

    (ends,) = call(finish_kernel, [two_b], [VMEM] * 7)(first, second, t1, from_low, from_high, g0, z0)
    (residual,) = call(residual_kernel, [full], [VMEM] * 5)(first, second, p, q0, w1)
    volume, gradient = call(
        place_kernel, [sds((ZD, L, X), F32)] * 2, [SMEM] + [VMEM] * 4
    )(me, *exchange((ends,) * 4))
    return volume, residual.reshape(projections.shape), gradient


def solution(mesh):
    in_specs = (
        P("ang", "slab", None, None),
        P("ang", None, None, None, None),
        P("ang", None, None),
        P("ang", "slab", None, None, None),
        P("ang", "slab", None),
    )
    out_specs = (P("slab", None, None), P("ang", "slab", None, None), P("slab", None, None))
    return jax.shard_map(
        per_device, mesh=mesh, in_specs=in_specs, out_specs=out_specs, check_vma=False
    )
```

```python
import functools

import jax
import jax.numpy as jnp
from jax import lax
from jax.experimental import pallas as pl
from jax.experimental.pallas import tpu as pltpu
from jax.sharding import PartitionSpec as P

F32 = jnp.float32
BF16 = jnp.bfloat16
ANG = 4
PAIR = 2
L = 16
X = 4096
Q = X // ANG
UB = 32
ZD = 4
CH = 128
COEF = 3 * 128
GROUP = 8
VMEM = pl.BlockSpec(memory_space=pltpu.VMEM)
SMEM = pl.BlockSpec(memory_space=pltpu.SMEM)
HBM = pl.BlockSpec(memory_space=pltpu.HBM)
MID = BF16
LIMIT = 48 * 1024 * 1024


def call(kernel, outs, specs, scratch=(), flops=0, nbytes=2_000_000):
    return pl.pallas_call(
        kernel,
        out_shape=outs,
        in_specs=specs,
        out_specs=[VMEM] * len(outs),
        scratch_shapes=list(scratch),
        compiler_params=pltpu.CompilerParams(vmem_limit_bytes=LIMIT),
        cost_estimate=pl.CostEstimate(flops=flops, bytes_accessed=nbytes, transcendentals=0),
    )


def sds(shape, dtype):
    return jax.ShapeDtypeStruct(shape, dtype)


def halves(value):
    high = value.astype(BF16)
    low = (value - high.astype(F32)).astype(BF16)
    return jnp.concatenate([high, low], axis=0)


def fold(value):
    total = value[:8] + value[8:]
    out = total[:, :128]
    for at in range(1, total.shape[1] // 128):
        out = out + total[:, 128 * at:128 * (at + 1)]
    return out


def weight_copies(w_hbm, w_buf, sem):
    return [
        pltpu.make_async_copy(
            w_hbm.at[a, pl.ds(GROUP * g, GROUP)], w_buf.at[a, pl.ds(GROUP * g, GROUP)],
            sem.at[a, g],
        )
        for a in range(PAIR)
        for g in range(UB // GROUP)
    ]


def window(cols, a, block):
    return pl.ds(pl.multiple_of(cols[a, block, 0] * 128, 128), 384)


def back_block(a, block, value, cols, w_buf, acc):
    both = halves(value)
    spread = lax.dot_general(
        both, w_buf[a, block], (((1,), (1,)), ((), ())), preferred_element_type=F32
    )
    at = window(cols, a, block)
    acc[a, :, at] += spread[:L] + spread[L:]


def send_shares(me, acc, outs):
    for r in range(ANG):
        quarter = lax.rem(me + r, ANG)
        share = acc[:, :, pl.ds(pl.multiple_of(quarter * Q, Q), Q)]
        outs[r][:, :, :Q] = share.astype(outs[r].dtype)


def back_kernel(me_ref, cols, stencil, p_ref, w_hbm, o0, o1, o2, o3, w_buf, acc, sem):
    copies = weight_copies(w_hbm, w_buf, sem)
    for copy in copies:
        copy.start()
    acc[...] = jnp.zeros_like(acc)
    for a in range(PAIR):
        for g in range(UB // GROUP):
            copies[a * (UB // GROUP) + g].wait()
            for i in range(GROUP):
                block = g * GROUP + i
                back_block(a, block, p_ref[a, :, 128 * block:128 * (block + 1)], cols, w_buf, acc)
    outs = (o0, o1, o2, o3)
    send_shares(me_ref[0], acc, outs)
    at_row = lax.broadcasted_iota(jnp.int32, (L, 128), 0)
    for i in range(PAIR):
        rest = jnp.zeros((L, 128), F32)
        for e in range(12):
            rest = jnp.where(at_row == e, stencil[12 * i + e], rest)
        for part in range(3):
            piece = rest.astype(BF16)
            rest = rest - piece.astype(F32)
            for out in outs:
                out[i, :, Q + 128 * part:Q + 128 * (part + 1)] = piece


def both_body(cols, copies, w_buf, acc, lhs, store):
    acc[...] = jnp.zeros_like(acc)
    for a in range(PAIR):
        for g in range(UB // GROUP):
            copies[a * (UB // GROUP) + g].wait()
            images = []
            for i in range(GROUP):
                block = g * GROUP + i
                image = jnp.dot(lhs(a, window(cols, a, block)), w_buf[a, block], preferred_element_type=F32)
                if image.shape[0] > L:
                    image = image[:L] + image[L:]
                store(a, block, image)
                images.append(image)
            for i in range(GROUP):
                back_block(a, g * GROUP + i, images[i], cols, w_buf, acc)


def gather_shares(me, shares, place):
    for r in range(ANG):
        quarter = lax.rem(me + ANG - r, ANG)
        place(pl.ds(pl.multiple_of(quarter * Q, Q), Q), shares[r])


def first_kernel(me_ref, cols, h0, h1, h2, h3, w_hbm, o0, o1, o2, o3, q_out, dots, hb, w_buf, acc, sem):
    copies = weight_copies(w_hbm, w_buf, sem)
    for copy in copies:
        copy.start()

    def place(at, share):
        hb[:, :, at] = share[...]

    def store(a, block, image):
        q_out[a, :, 128 * block:128 * (block + 1)] = image

    gather_shares(me_ref[0], (h0, h1, h2, h3), place)
    both_body(cols, copies, w_buf, acc, lambda a, at: hb[a, :, at], store)
    send_shares(me_ref[0], acc, (o0, o1, o2, o3))
    dots[...] = fold(q_out[0] * q_out[0]) + fold(q_out[1] * q_out[1])


def second_kernel(me_ref, cols, h0, h1, h2, h3, q0_ref, gamma_ref, curve_ref, inner_ref, w_hbm,
                  o0, o1, o2, o3, w_out, sums, both, w_buf, acc, sem):
    copies = weight_copies(w_hbm, w_buf, sem)
    for copy in copies:
        copy.start()

    def place(at, share):
        for a in range(PAIR):
            both[a, :, at] = halves(share[a].astype(F32))

    def store(a, block, image):
        w_out[a, :, 128 * block:128 * (block + 1)] = image

    gather_shares(me_ref[0], (h0, h1, h2, h3), place)
    both_body(cols, copies, w_buf, acc, lambda a, at: both[a, :, at], store)
    send_shares(me_ref[0], acc, (o0, o1, o2, o3))
    cross = fold(w_out[0] * q0_ref[0]) + fold(w_out[1] * q0_ref[1])
    own = fold(w_out[0] * w_out[0]) + fold(w_out[1] * w_out[1])
    lane = lax.broadcasted_iota(jnp.int32, (1, 128), 1)
    row = jnp.zeros((1, 128), F32)
    for at, value in enumerate((gamma_ref[...], curve_ref[...], inner_ref[:8], inner_ref[8:], cross, own)):
        row = jnp.where(lane == at, jnp.sum(value), row)
    sums[...] = row


def spread_slices(coefs, parts, cut):
    totals = [None] * 12
    for r in range(ANG):
        for i in range(PAIR):
            value = parts[r][i, :, cut].astype(F32)
            for e in range(12):
                term = coefs[r, i, e:e + 1, :] * value
                totals[e] = term if totals[e] is None else totals[e] + term
    return totals


def cuts():
    return [pl.ds(at * CH, CH) for at in range(Q // CH)]


def combine_parts(coefs, parts, t1, up, down, up_far, down_far):
    for cut in cuts():
        totals = spread_slices(coefs, parts, cut)
        for z in range(ZD):
            below, own, above = totals[z], totals[4 + z], totals[8 + z]
            t1[z, :, cut] = own
            up[z, :, cut] = own.astype(BF16)
            down[z, :, cut] = own.astype(BF16)
            up[4 + z, :, cut] = above.astype(BF16)
            down[4 + z, :, cut] = below.astype(BF16)
            up_far[z, :, cut] = above.astype(BF16)
            down_far[z, :, cut] = below.astype(BF16)


def open_kernel(c0, c1, c2, c3, t1, up, down, up_far, down_far, coefs):
    parts = (c0, c1, c2, c3)
    for r in range(ANG):
        for i in range(PAIR):
            value = parts[r][i, :, Q:Q + 128].astype(F32)
            value = value + parts[r][i, :, Q + 128:Q + 256].astype(F32)
            coefs[r, i] = value + parts[r][i, :, Q + 256:].astype(F32)
    combine_parts(coefs, parts, t1, up, down, up_far, down_far)


def combine_kernel(coefs, c0, c1, c2, c3, t1, up, down, up_far, down_far):
    combine_parts(coefs, (c0, c1, c2, c3), t1, up, down, up_far, down_far)


def pieces_body(coefs, t1, up, down, from_low, from_high, far_low, far_high, g_out, outs, note):
    for cut in cuts():
        def get(ref, z):
            return ref[z, :, cut].astype(F32)

        cells = []
        for z in range(ZD):
            cells.append(get(from_low, z) + get(far_low, z) + get(down, 4 + z))
        for z in range(ZD):
            value = t1[z, :, cut] + get(from_low, 4 + z) + get(from_high, 4 + z)
            g_out[z, :, cut] = value
            note(z, cut, value)
            cells.append(value)
        for z in range(ZD):
            cells.append(get(from_high, z) + get(far_high, z) + get(up, 4 + z))
        for r in range(ANG):
            for i in range(PAIR):
                total = None
                for e in range(12):
                    term = coefs[(ANG - r) % ANG, i, e:e + 1, :] * cells[e]
                    total = term if total is None else total + term
                outs[r][i, :, cut] = total.astype(outs[r].dtype)


def pieces_first(coefs, t1, up, down, from_low, from_high, far_low, far_high,
                 g_out, h0, h1, h2, h3, dots):
    kept = [jnp.zeros((8, 128), F32)]

    def note(z, cut, value):
        kept[0] = kept[0] + fold(value * value)

    pieces_body(coefs, t1, up, down, from_low, from_high, far_low, far_high, g_out, (h0, h1, h2, h3), note)
    dots[...] = kept[0]


def pieces_second(coefs, g0, t1, up, down, from_low, from_high, far_low, far_high,
                  g_out, h0, h1, h2, h3, dots):
    kept = [jnp.zeros((8, 128), F32)] * 2

    def note(z, cut, value):
        kept[0] = kept[0] + fold(value * g0[z, :, cut])
        kept[1] = kept[1] + fold(value * value)

    pieces_body(coefs, t1, up, down, from_low, from_high, far_low, far_high, g_out, (h0, h1, h2, h3), note)
    dots[:8] = kept[0]
    dots[8:] = kept[1]


def last_kernel(coefs, c0, c1, c2, c3, t1, up, down):
    for cut in cuts():
        totals = spread_slices(coefs, (c0, c1, c2, c3), cut)
        for z in range(ZD):
            down[z, :, cut] = totals[z].astype(down.dtype)
            t1[z, :, cut] = totals[4 + z]
            up[z, :, cut] = totals[8 + z].astype(up.dtype)


def steps(sums_ref):
    total = sums_ref[0]
    for at in range(1, sums_ref.shape[0]):
        total = total + sums_ref[at]
    lane = lax.broadcasted_iota(jnp.int32, (1, 128), 1)
    gamma0, curve0, inner, norm, cross, own = [
        jnp.sum(jnp.where(lane == at, total, 0.0)) for at in range(6)
    ]
    step0 = gamma0 / curve0
    gamma1 = gamma0 - 2.0 * step0 * inner + step0 * step0 * norm
    ratio = gamma1 / gamma0
    curve1 = (1.0 + ratio) * (1.0 + ratio) * curve0 - 2.0 * (1.0 + ratio) * step0 * cross + step0 * step0 * own
    step1 = gamma1 / curve1
    return step0 + step1 * (1.0 + ratio), step0 * step1


def volume_kernel(sums, g0, z0, out):
    one, two = steps(sums)
    for z in range(ZD):
        out[z] = (one * g0[z] - two * z0[z]).astype(BF16)


def gradient_kernel(sums, t1, from_low, from_high, g0, z0, out):
    one, two = steps(sums)
    for z in range(ZD):
        last = t1[z] + from_low[z].astype(F32) + from_high[z].astype(F32)
        out[z] = (g0[z] - one * z0[z] + two * last).astype(BF16)


def residual_kernel(sums, p, q0, w0, out):
    one, two = steps(sums)
    for a in range(PAIR):
        out[a] = p[a] - one * q0[a] + two * w0[a]


def place_kernel(me_ref, s0, s1, s2, s3, out):
    def place(at, share):
        out[:, :, at] = share[...].astype(F32)

    gather_shares(me_ref[0], (s0, s1, s2, s3), place)


def along_ang(value, steps):
    return lax.ppermute(value, "ang", [(i, (i + steps) % ANG) for i in range(ANG)])


def along_slab(value, steps):
    count = lax.axis_size("slab")
    pairs = [(i, i + steps) for i in range(count) if 0 <= i + steps < count]
    return lax.ppermute(value, "slab", pairs)


def exchange(shares):
    far = along_ang(shares[2], 2)
    near = along_ang(shares[1], 1)
    back = along_ang(shares[3], 3)
    return (shares[0], near, far, back)


def per_device(projections, weights, columns, row_weights, reach):
    rows = row_weights[:, 0, :, 0, :]
    below = rows[:, 0] * (reach[:, 0, :1] == -1).astype(F32)
    above = rows[:, 2] * (reach[:, 0, 1:] == 1).astype(F32)
    stencil = jnp.stack([along_slab(above, 1), rows[:, 1], along_slab(below, -1)], axis=1).reshape(PAIR * 12)

    me = lax.axis_index("ang").astype(jnp.int32).reshape(1)
    w = weights.reshape(PAIR, UB, 384, 128)
    p = projections.reshape(PAIR, L, X)

    def share(dtype, more=0):
        return sds((PAIR, L, Q + more), dtype)

    full = sds((PAIR, L, X), F32)
    part = sds((ZD, L, Q), F32)
    part_b = sds((ZD, L, Q), BF16)
    two_b = sds((2 * ZD, L, Q), BF16)
    w_scratch = [
        pltpu.VMEM((PAIR, UB, 384, 128), BF16),
        pltpu.VMEM((PAIR, L, X), F32),
        pltpu.SemaphoreType.DMA((PAIR, UB // GROUP)),
    ]
    macs = 2 * PAIR * L * UB * 384 * 128
    sent = [part, two_b, two_b, part_b, part_b]

    def halo(t1, up, down, up_far, down_far):
        return (t1, up, down, along_slab(up, 1), along_slab(down, -1),
                along_slab(up_far, 2), along_slab(down_far, -2))

    shares = call(
        back_kernel, [share(BF16, COEF)] * 4, [SMEM] * 3 + [VMEM, HBM], w_scratch, flops=2 * macs, nbytes=7_000_000
    )(me, columns, stencil, p, w)
    *spread, coefs = call(
        open_kernel, sent + [sds((ANG, PAIR, L, 128), F32)], [VMEM] * 4, flops=10_000_000
    )(*exchange(shares))
    g0, *shares, gamma = call(
        pieces_first, [part] + [share(BF16)] * 4 + [sds((8, 128), F32)], [VMEM] * 8, flops=10_000_000
    )(coefs, *halo(*spread))

    *shares, q0, curve = call(
        first_kernel, [share(MID)] * 4 + [full, sds((8, 128), F32)],
        [SMEM] * 2 + [VMEM] * 4 + [HBM], [pltpu.VMEM((PAIR, L, X), BF16)] + w_scratch,
        flops=3 * macs, nbytes=7_000_000,
    )(me, columns, *exchange(shares), w)
    spread = call(combine_kernel, sent, [VMEM] * 5, flops=10_000_000)(coefs, *exchange(shares))
    z0, *shares, inner = call(
        pieces_second, [part] + [share(F32)] * 4 + [sds((16, 128), F32)], [VMEM] * 9, flops=10_000_000
    )(coefs, g0, *halo(*spread))

    *shares, w0, sums = call(
        second_kernel, [share(F32)] * 4 + [full, sds((1, 128), F32)],
        [SMEM] * 2 + [VMEM] * 8 + [HBM], [pltpu.VMEM((PAIR, 2 * L, X), BF16)] + w_scratch,
        flops=4 * macs, nbytes=9_000_000,
    )(me, columns, *exchange(shares), q0, gamma, curve, inner, w)
    shares = exchange(shares)
    count = lax.axis_size("slab") * ANG
    sums = lax.all_to_all(jnp.broadcast_to(sums[None], (count, 1, 128)), ("slab", "ang"), 0, 0, tiled=True)
    (volume,) = call(volume_kernel, [part_b], [VMEM] * 3)(sums, g0, z0)
    (residual,) = call(residual_kernel, [full], [VMEM] * 4)(sums, p, q0, w0)
    volume = exchange((volume,) * 4)
    t1, up, down = call(last_kernel, [part] * 3, [VMEM] * 5, flops=10_000_000)(coefs, *shares)
    (gradient,) = call(gradient_kernel, [part_b], [VMEM] * 6)(
        sums, t1, along_slab(up, 1), along_slab(down, -1), g0, z0
    )
    whole = [sds((ZD, L, X), F32)]
    (volume,) = call(place_kernel, whole, [SMEM] + [VMEM] * 4)(me, *volume)
    (gradient,) = call(place_kernel, whole, [SMEM] + [VMEM] * 4)(me, *exchange((gradient,) * 4))
    return volume, residual.reshape(projections.shape), gradient


def solution(mesh):
    in_specs = (
        P("ang", "slab", None, None),
        P("ang", None, None, None, None),
        P("ang", None, None),
        P("ang", "slab", None, None, None),
        P("ang", "slab", None),
    )
    out_specs = (P("slab", None, None), P("ang", "slab", None, None), P("slab", None, None))
    return jax.shard_map(
        per_device, mesh=mesh, in_specs=in_specs, out_specs=out_specs, check_vma=False
    )
```

```python
import functools

import jax
import jax.numpy as jnp
from jax import lax
from jax.experimental import pallas as pl
from jax.experimental.pallas import tpu as pltpu
from jax.sharding import PartitionSpec as P

F32 = jnp.float32
BF16 = jnp.bfloat16
ANG = 4
PAIR = 2
L = 16
X = 4096
Q = X // ANG
UB = 32
ZD = 4
CH = 128
COEF = 3 * 128
GROUP = 8
VMEM = pl.BlockSpec(memory_space=pltpu.VMEM)
SMEM = pl.BlockSpec(memory_space=pltpu.SMEM)
MID = BF16
HBM = pl.BlockSpec(memory_space=pltpu.HBM)


def call(kernel, outs, specs, scratch=(), flops=0, nbytes=2_000_000, limit=24):
    return pl.pallas_call(
        kernel,
        out_shape=outs,
        in_specs=specs,
        out_specs=[VMEM] * len(outs),
        scratch_shapes=list(scratch),
        compiler_params=pltpu.CompilerParams(vmem_limit_bytes=limit * 1024 * 1024),
        cost_estimate=pl.CostEstimate(flops=flops, bytes_accessed=nbytes, transcendentals=0),
    )


def sds(shape, dtype):
    return jax.ShapeDtypeStruct(shape, dtype)


def halves(value):
    high = value.astype(BF16)
    low = (value - high.astype(F32)).astype(BF16)
    return jnp.concatenate([high, low], axis=0)


def fold(value):
    total = value[:8] + value[8:]
    out = total[:, :128]
    for at in range(1, total.shape[1] // 128):
        out = out + total[:, 128 * at:128 * (at + 1)]
    return out


def window(cols, a, block):
    return pl.ds(pl.multiple_of(cols[0, a, block] * 128, 128), 384)


def back_block(a, block, value, cols, w, acc):
    both = halves(value)
    spread = lax.dot_general(
        both, w[a, block], (((1,), (1,)), ((), ())), preferred_element_type=F32
    )
    at = window(cols, a, block)
    acc[a, :, at] += spread[:L] + spread[L:]


def send_shares(me, acc, outs):
    for r in range(ANG):
        quarter = lax.rem(me + r, ANG)
        share = acc[:, :, pl.ds(pl.multiple_of(quarter * Q, Q), Q)]
        outs[r][:, :, :Q] = share.astype(outs[r].dtype)


def mask_kernel(rows, reach, above, below):
    for i in range(PAIR):
        for z in range(ZD):
            top = jnp.where(reach[i, 0, 1] == 1, rows[i, 0, 2, 0, z], 0.0)
            low = jnp.where(reach[i, 0, 0] == -1, rows[i, 0, 0, 0, z], 0.0)
            above[ZD * i + z:ZD * i + z + 1] = jnp.full((1, 128), top, F32)
            below[ZD * i + z:ZD * i + z + 1] = jnp.full((1, 128), low, F32)


def back_kernel(me_ref, cols, rows, from_low, from_high, p_ref, w_hbm, o0, o1, o2, o3, w, acc, sem):
    copies = {}
    for a in range(PAIR):
        for g in range(UB // GROUP):
            span = pl.ds(GROUP * g, GROUP)
            copies[a, g] = pltpu.make_async_copy(w_hbm.at[a, span], w.at[a, span], sem.at[a, g])
            copies[a, g].start()
    acc[...] = jnp.zeros_like(acc)
    for a in range(PAIR):
        for block in range(UB):
            if block % GROUP == 0:
                copies[a, block // GROUP].wait()
            back_block(a, block, p_ref[a, 0, :, 128 * block:128 * (block + 1)], cols, w, acc)
    outs = (o0, o1, o2, o3)
    send_shares(me_ref[0], acc, outs)
    for i in range(PAIR):
        own = [jnp.full((1, 128), rows[i, 0, 1, 0, z], F32) for z in range(ZD)]
        rest = jnp.concatenate(
            [from_low[ZD * i:ZD * (i + 1)]] + own + [from_high[ZD * i:ZD * (i + 1)], jnp.zeros((4, 128), F32)], axis=0
        )
        for part in range(3):
            piece = rest.astype(BF16)
            rest = rest - piece.astype(F32)
            for out in outs:
                out[i, :, Q + 128 * part:Q + 128 * (part + 1)] = piece


def both_body(cols, w, acc, lhs, store):
    acc[...] = jnp.zeros_like(acc)
    for a in range(PAIR):
        for g in range(UB // GROUP):
            images = []
            for i in range(GROUP):
                block = g * GROUP + i
                image = jnp.dot(lhs(a, window(cols, a, block)), w[a, block], preferred_element_type=F32)
                if image.shape[0] > L:
                    image = image[:L] + image[L:]
                store(a, block, image)
                images.append(image)
            for i in range(GROUP):
                back_block(a, g * GROUP + i, images[i], cols, w, acc)


def gather_shares(me, shares, place):
    for r in range(ANG):
        quarter = lax.rem(me + ANG - r, ANG)
        place(pl.ds(pl.multiple_of(quarter * Q, Q), Q), shares[r])


def first_kernel(me_ref, cols, h0, h1, h2, h3, w, o0, o1, o2, o3, q_out, dots, hb, acc):

    def place(at, share):
        hb[:, :, at] = share[...]

    def store(a, block, image):
        q_out[a, :, 128 * block:128 * (block + 1)] = image

    gather_shares(me_ref[0], (h0, h1, h2, h3), place)
    both_body(cols, w, acc, lambda a, at: hb[a, :, at], store)
    send_shares(me_ref[0], acc, (o0, o1, o2, o3))
    dots[...] = fold(q_out[0] * q_out[0]) + fold(q_out[1] * q_out[1])


def second_kernel(me_ref, cols, h0, h1, h2, h3, q0_ref, gamma_ref, curve_ref, inner_ref, w,
                  o0, o1, o2, o3, w_out, sums, both, acc):

    def place(at, share):
        for a in range(PAIR):
            both[a, :, at] = halves(share[a].astype(F32))

    def store(a, block, image):
        w_out[a, :, 128 * block:128 * (block + 1)] = image

    gather_shares(me_ref[0], (h0, h1, h2, h3), place)
    both_body(cols, w, acc, lambda a, at: both[a, :, at], store)
    send_shares(me_ref[0], acc, (o0, o1, o2, o3))
    cross = fold(w_out[0] * q0_ref[0]) + fold(w_out[1] * q0_ref[1])
    own = fold(w_out[0] * w_out[0]) + fold(w_out[1] * w_out[1])
    lane = lax.broadcasted_iota(jnp.int32, (1, 128), 1)
    row = jnp.zeros((1, 128), F32)
    for at, value in enumerate((gamma_ref[...], curve_ref[...], inner_ref[:8], inner_ref[8:], cross, own)):
        row = jnp.where(lane == at, jnp.sum(value), row)
    sums[...] = jnp.broadcast_to(row[None], sums.shape)


def spread_slices(coefs, parts, cut):
    totals = [None] * 12
    for r in range(ANG):
        for i in range(PAIR):
            value = parts[r][i, :, cut].astype(F32)
            for e in range(12):
                term = coefs[r, i, e:e + 1, :] * value
                totals[e] = term if totals[e] is None else totals[e] + term
    return totals


def cuts():
    return [pl.ds(at * CH, CH) for at in range(Q // CH)]


def combine_parts(coefs, parts, t1, up, down, up_far, down_far):
    for cut in cuts():
        totals = spread_slices(coefs, parts, cut)
        for z in range(ZD):
            below, own, above = totals[z], totals[4 + z], totals[8 + z]
            t1[z, :, cut] = own
            up[z, :, cut] = own.astype(BF16)
            down[z, :, cut] = own.astype(BF16)
            up[4 + z, :, cut] = above.astype(BF16)
            down[4 + z, :, cut] = below.astype(BF16)
            up_far[z, :, cut] = above.astype(BF16)
            down_far[z, :, cut] = below.astype(BF16)


def open_kernel(c0, c1, c2, c3, t1, up, down, up_far, down_far, coefs):
    parts = (c0, c1, c2, c3)
    for r in range(ANG):
        for i in range(PAIR):
            value = parts[r][i, :, Q:Q + 128].astype(F32)
            value = value + parts[r][i, :, Q + 128:Q + 256].astype(F32)
            coefs[r, i] = value + parts[r][i, :, Q + 256:].astype(F32)
    combine_parts(coefs, parts, t1, up, down, up_far, down_far)


def combine_kernel(coefs, c0, c1, c2, c3, t1, up, down, up_far, down_far):
    combine_parts(coefs, (c0, c1, c2, c3), t1, up, down, up_far, down_far)


def pieces_body(coefs, t1, up, down, from_low, from_high, far_low, far_high, g_out, outs, note):
    for cut in cuts():
        def get(ref, z):
            return ref[z, :, cut].astype(F32)

        cells = []
        for z in range(ZD):
            cells.append(get(from_low, z) + get(far_low, z) + get(down, 4 + z))
        for z in range(ZD):
            value = t1[z, :, cut] + get(from_low, 4 + z) + get(from_high, 4 + z)
            g_out[z, :, cut] = value
            note(z, cut, value)
            cells.append(value)
        for z in range(ZD):
            cells.append(get(from_high, z) + get(far_high, z) + get(up, 4 + z))
        for r in range(ANG):
            for i in range(PAIR):
                total = None
                for e in range(12):
                    term = coefs[(ANG - r) % ANG, i, e:e + 1, :] * cells[e]
                    total = term if total is None else total + term
                outs[r][i, :, cut] = total.astype(outs[r].dtype)


def pieces_first(coefs, t1, up, down, from_low, from_high, far_low, far_high,
                 g_out, h0, h1, h2, h3, dots):
    kept = [jnp.zeros((8, 128), F32)]

    def note(z, cut, value):
        kept[0] = kept[0] + fold(value * value)

    pieces_body(coefs, t1, up, down, from_low, from_high, far_low, far_high, g_out, (h0, h1, h2, h3), note)
    dots[...] = kept[0]


def pieces_second(coefs, g0, t1, up, down, from_low, from_high, far_low, far_high,
                  g_out, h0, h1, h2, h3, dots):
    kept = [jnp.zeros((8, 128), F32)] * 2

    def note(z, cut, value):
        kept[0] = kept[0] + fold(value * g0[z, :, cut])
        kept[1] = kept[1] + fold(value * value)

    pieces_body(coefs, t1, up, down, from_low, from_high, far_low, far_high, g_out, (h0, h1, h2, h3), note)
    dots[:8] = kept[0]
    dots[8:] = kept[1]


def last_kernel(coefs, c0, c1, c2, c3, t1, up, down):
    for cut in cuts():
        totals = spread_slices(coefs, (c0, c1, c2, c3), cut)
        for z in range(ZD):
            down[z, :, cut] = totals[z].astype(down.dtype)
            t1[z, :, cut] = totals[4 + z]
            up[z, :, cut] = totals[8 + z].astype(up.dtype)


def steps(sums_ref):
    total = sums_ref[0]
    for at in range(1, sums_ref.shape[0]):
        total = total + sums_ref[at]
    lane = lax.broadcasted_iota(jnp.int32, (1, 128), 1)
    gamma0, curve0, inner, norm, cross, own = [
        jnp.sum(jnp.where(lane == at, total, 0.0)) for at in range(6)
    ]
    step0 = gamma0 / curve0
    gamma1 = gamma0 - 2.0 * step0 * inner + step0 * step0 * norm
    ratio = gamma1 / gamma0
    curve1 = (1.0 + ratio) * (1.0 + ratio) * curve0 - 2.0 * (1.0 + ratio) * step0 * cross + step0 * step0 * own
    step1 = gamma1 / curve1
    return step0 + step1 * (1.0 + ratio), step0 * step1


def volume_kernel(sums, g0, z0, out):
    one, two = steps(sums)
    for z in range(ZD):
        out[z] = (one * g0[z] - two * z0[z]).astype(BF16)


def gradient_kernel(sums, t1, from_low, from_high, g0, z0, out):
    one, two = steps(sums)
    for z in range(ZD):
        last = t1[z] + from_low[z].astype(F32) + from_high[z].astype(F32)
        out[z] = (g0[z] - one * z0[z] + two * last).astype(BF16)


def residual_kernel(sums, p, q0, w0, out):
    one, two = steps(sums)
    for a in range(PAIR):
        out[a, 0] = p[a, 0] - one * q0[a] + two * w0[a]


def place_kernel(me_ref, s0, s1, s2, s3, out):
    def place(at, share):
        out[:, :, at] = share[...].astype(F32)

    gather_shares(me_ref[0], (s0, s1, s2, s3), place)


def along_ang(value, steps):
    return lax.ppermute(value, "ang", [(i, (i + steps) % ANG) for i in range(ANG)])


def along_slab(value, steps):
    count = lax.axis_size("slab")
    pairs = [(i, i + steps) for i in range(count) if 0 <= i + steps < count]
    return lax.ppermute(value, "slab", pairs)


def exchange(shares):
    far = along_ang(shares[2], 2)
    near = along_ang(shares[1], 1)
    back = along_ang(shares[3], 3)
    return (shares[0], near, far, back)


def per_device(projections, weights, columns, row_weights, reach):
    row = sds((PAIR * ZD, 128), F32)
    above, below = call(mask_kernel, [row] * 2, [SMEM] * 2)(row_weights, reach)
    edges = (along_slab(above, 1), along_slab(below, -1))

    me = lax.axis_index("ang").astype(jnp.int32).reshape(1)
    cols = columns.transpose(2, 0, 1)

    def share(dtype, more=0):
        return sds((PAIR, L, Q + more), dtype)

    full = sds((PAIR, L, X), F32)
    part = sds((ZD, L, Q), F32)
    part_b = sds((ZD, L, Q), BF16)
    two_b = sds((2 * ZD, L, Q), BF16)
    acc = pltpu.VMEM((PAIR, L, X), F32)
    macs = 2 * PAIR * L * UB * 384 * 128
    sent = [part, two_b, two_b, part_b, part_b]

    def halo(t1, up, down, up_far, down_far):
        return (t1, up, down, along_slab(up, 1), along_slab(down, -1),
                along_slab(up_far, 2), along_slab(down_far, -2))

    *shares, w = call(
        back_kernel, [share(BF16, COEF)] * 4 + [sds((PAIR, UB, 384, 128), BF16)],
        [SMEM] * 3 + [VMEM] * 3 + [HBM], [acc, pltpu.SemaphoreType.DMA((PAIR, UB // GROUP))],
        flops=2 * macs, nbytes=7_000_000, limit=46,
    )(me, cols, row_weights, *edges, projections, weights.reshape(PAIR, UB, 384, 128))
    *spread, coefs = call(
        open_kernel, sent + [sds((ANG, PAIR, L, 128), F32)], [VMEM] * 4, flops=10_000_000
    )(*exchange(shares))
    g0, *shares, gamma = call(
        pieces_first, [part] + [share(BF16)] * 4 + [sds((8, 128), F32)], [VMEM] * 8, flops=10_000_000
    )(coefs, *halo(*spread))

    *shares, q0, curve = call(
        first_kernel, [share(MID)] * 4 + [full, sds((8, 128), F32)],
        [SMEM] * 2 + [VMEM] * 5, [pltpu.VMEM((PAIR, L, X), BF16), acc],
        flops=3 * macs, nbytes=7_000_000,
    )(me, cols, *exchange(shares), w)
    spread = call(combine_kernel, sent, [VMEM] * 5, flops=10_000_000)(coefs, *exchange(shares))
    z0, *shares, inner = call(
        pieces_second, [part] + [share(F32)] * 4 + [sds((16, 128), F32)], [VMEM] * 9, flops=10_000_000
    )(coefs, g0, *halo(*spread))

    *shares, w0, sums = call(
        second_kernel, [share(F32)] * 4 + [full, sds((lax.axis_size("slab") * ANG, 1, 128), F32)],
        [SMEM] * 2 + [VMEM] * 9, [pltpu.VMEM((PAIR, 2 * L, X), BF16), acc],
        flops=4 * macs, nbytes=9_000_000,
    )(me, cols, *exchange(shares), q0, gamma, curve, inner, w)
    shares = exchange(shares)
    sums = lax.all_to_all(sums, ("slab", "ang"), 0, 0, tiled=True)
    (volume,) = call(volume_kernel, [part_b], [VMEM] * 3)(sums, g0, z0)
    (residual,) = call(residual_kernel, [sds(projections.shape, F32)], [VMEM] * 4)(sums, projections, q0, w0)
    volume = exchange((volume,) * 4)
    t1, up, down = call(last_kernel, [part] * 3, [VMEM] * 5, flops=10_000_000)(coefs, *shares)
    (gradient,) = call(gradient_kernel, [part_b], [VMEM] * 6)(
        sums, t1, along_slab(up, 1), along_slab(down, -1), g0, z0
    )
    whole = [sds((ZD, L, X), F32)]
    (volume,) = call(place_kernel, whole, [SMEM] + [VMEM] * 4)(me, *volume)
    (gradient,) = call(place_kernel, whole, [SMEM] + [VMEM] * 4)(me, *exchange((gradient,) * 4))
    return volume, residual, gradient


def solution(mesh):
    in_specs = (
        P("ang", "slab", None, None),
        P("ang", None, None, None, None),
        P("ang", None, None),
        P("ang", "slab", None, None, None),
        P("ang", "slab", None),
    )
    out_specs = (P("slab", None, None), P("ang", "slab", None, None), P("slab", None, None))
    return jax.shard_map(
        per_device, mesh=mesh, in_specs=in_specs, out_specs=out_specs, check_vma=False
    )
```

```python
import functools

import jax
import jax.numpy as jnp
from jax import lax
from jax.experimental import pallas as pl
from jax.experimental.pallas import tpu as pltpu
from jax.sharding import PartitionSpec as P

F32 = jnp.float32
BF16 = jnp.bfloat16
ANG = 4
PAIR = 2
L = 16
X = 4096
Q = X // ANG
UB = 32
ZD = 4
CH = 128
COEF = 3 * 128
GROUP = 8
VMEM = pl.BlockSpec(memory_space=pltpu.VMEM)
SMEM = pl.BlockSpec(memory_space=pltpu.SMEM)
MID = BF16
HBM = pl.BlockSpec(memory_space=pltpu.HBM)


def call(kernel, outs, specs, scratch=(), flops=0, nbytes=2_000_000, limit=24):
    return pl.pallas_call(
        kernel,
        out_shape=outs,
        in_specs=specs,
        out_specs=[VMEM] * len(outs),
        scratch_shapes=list(scratch),
        compiler_params=pltpu.CompilerParams(vmem_limit_bytes=limit * 1024 * 1024),
        cost_estimate=pl.CostEstimate(flops=flops, bytes_accessed=nbytes, transcendentals=0),
    )


def sds(shape, dtype):
    return jax.ShapeDtypeStruct(shape, dtype)


def halves(value):
    high = value.astype(BF16)
    low = (value - high.astype(F32)).astype(BF16)
    return jnp.concatenate([high, low], axis=0)


def fold(value):
    total = value[:8] + value[8:]
    out = total[:, :128]
    for at in range(1, total.shape[1] // 128):
        out = out + total[:, 128 * at:128 * (at + 1)]
    return out


def window(cols, a, block):
    return pl.ds(pl.multiple_of(cols[0, a, block] * 128, 128), 384)


def back_block(a, block, value, cols, w, acc):
    both = halves(value)
    spread = lax.dot_general(
        both, w[a, block], (((1,), (1,)), ((), ())), preferred_element_type=F32
    )
    at = window(cols, a, block)
    acc[a, :, at] += spread[:L] + spread[L:]


def send_shares(me, acc, outs):
    for r in range(ANG):
        quarter = me ^ r
        share = acc[:, :, pl.ds(pl.multiple_of(quarter * Q, Q), Q)]
        outs[r][:, :, :Q] = share.astype(outs[r].dtype)


def mask_kernel(me, rows, reach, inner, outer):
    even = me[1] == 0
    for i in range(PAIR):
        for z in range(ZD):
            top = jnp.where(reach[i, 0, 1] == 1, rows[i, 0, 2, 0, z], 0.0)
            low = jnp.where(reach[i, 0, 0] == -1, rows[i, 0, 0, 0, z], 0.0)
            at = slice(ZD * i + z, ZD * i + z + 1)
            inner[at] = jnp.full((1, 128), jnp.where(even, top, low), F32)
            outer[at] = jnp.full((1, 128), jnp.where(even, low, top), F32)


def back_kernel(me_ref, cols, rows, inner, outer, p_ref, w_hbm, o0, o1, o2, o3, w, acc, sem):
    copies = {}
    for a in range(PAIR):
        for g in range(UB // GROUP):
            span = pl.ds(GROUP * g, GROUP)
            copies[a, g] = pltpu.make_async_copy(w_hbm.at[a, span], w.at[a, span], sem.at[a, g])
            copies[a, g].start()
    acc[...] = jnp.zeros_like(acc)
    for a in range(PAIR):
        for block in range(UB):
            if block % GROUP == 0:
                copies[a, block // GROUP].wait()
            back_block(a, block, p_ref[a, 0, :, 128 * block:128 * (block + 1)], cols, w, acc)
    outs = (o0, o1, o2, o3)
    send_shares(me_ref[0], acc, outs)
    even = me_ref[1] == 0
    from_low = jnp.where(even, outer[...], inner[...])
    from_high = jnp.where(even, inner[...], outer[...])
    for i in range(PAIR):
        own = [jnp.full((1, 128), rows[i, 0, 1, 0, z], F32) for z in range(ZD)]
        rest = jnp.concatenate(
            [from_low[ZD * i:ZD * (i + 1)]] + own + [from_high[ZD * i:ZD * (i + 1)], jnp.zeros((4, 128), F32)], axis=0
        )
        for part in range(3):
            piece = rest.astype(BF16)
            rest = rest - piece.astype(F32)
            for out in outs:
                out[i, :, Q + 128 * part:Q + 128 * (part + 1)] = piece


def both_body(cols, w, acc, lhs, store):
    acc[...] = jnp.zeros_like(acc)
    for a in range(PAIR):
        for g in range(UB // GROUP):
            images = []
            for i in range(GROUP):
                block = g * GROUP + i
                image = jnp.dot(lhs(a, window(cols, a, block)), w[a, block], preferred_element_type=F32)
                if image.shape[0] > L:
                    image = image[:L] + image[L:]
                store(a, block, image)
                images.append(image)
            for i in range(GROUP):
                back_block(a, g * GROUP + i, images[i], cols, w, acc)


def gather_shares(me, shares, place):
    for r in range(ANG):
        quarter = me ^ r
        place(pl.ds(pl.multiple_of(quarter * Q, Q), Q), shares[r])


def first_kernel(me_ref, cols, h0, h1, h2, h3, w, o0, o1, o2, o3, q_out, dots, hb, acc):

    def place(at, share):
        hb[:, :, at] = share[...]

    def store(a, block, image):
        q_out[a, :, 128 * block:128 * (block + 1)] = image

    gather_shares(me_ref[0], (h0, h1, h2, h3), place)
    both_body(cols, w, acc, lambda a, at: hb[a, :, at], store)
    send_shares(me_ref[0], acc, (o0, o1, o2, o3))
    dots[...] = fold(q_out[0] * q_out[0]) + fold(q_out[1] * q_out[1])


def second_kernel(me_ref, cols, h0, h1, h2, h3, q0_ref, gamma_ref, curve_ref, inner_ref, w,
                  o0, o1, o2, o3, w_out, sums, both, acc):

    def place(at, share):
        for a in range(PAIR):
            both[a, :, at] = halves(share[a].astype(F32))

    def store(a, block, image):
        w_out[a, :, 128 * block:128 * (block + 1)] = image

    gather_shares(me_ref[0], (h0, h1, h2, h3), place)
    both_body(cols, w, acc, lambda a, at: both[a, :, at], store)
    send_shares(me_ref[0], acc, (o0, o1, o2, o3))
    cross = fold(w_out[0] * q0_ref[0]) + fold(w_out[1] * q0_ref[1])
    own = fold(w_out[0] * w_out[0]) + fold(w_out[1] * w_out[1])
    lane = lax.broadcasted_iota(jnp.int32, (1, 128), 1)
    row = jnp.zeros((1, 128), F32)
    for at, value in enumerate((gamma_ref[...], curve_ref[...], inner_ref[:8], inner_ref[8:], cross, own)):
        row = jnp.where(lane == at, jnp.sum(value), row)
    sums[...] = jnp.broadcast_to(row[None], sums.shape)


def spread_slices(coefs, parts, cut):
    totals = [None] * 12
    for r in range(ANG):
        for i in range(PAIR):
            value = parts[r][i, :, cut].astype(F32)
            for e in range(12):
                term = coefs[r, i, e:e + 1, :] * value
                totals[e] = term if totals[e] is None else totals[e] + term
    return totals


def cuts():
    return [pl.ds(at * CH, CH) for at in range(Q // CH)]


def combine_parts(coefs, parts, mine, sent):
    for cut in cuts():
        for e, total in enumerate(spread_slices(coefs, parts, cut)):
            mine[e, :, cut] = total
            sent[e, :, cut] = total.astype(BF16)


def open_kernel(c0, c1, c2, c3, mine, sent, coefs):
    parts = (c0, c1, c2, c3)
    for r in range(ANG):
        for i in range(PAIR):
            value = parts[r][i, :, Q:Q + 128].astype(F32)
            value = value + parts[r][i, :, Q + 128:Q + 256].astype(F32)
            coefs[r, i] = value + parts[r][i, :, Q + 256:].astype(F32)
    combine_parts(coefs, parts, mine, sent)


def combine_kernel(coefs, c0, c1, c2, c3, mine, sent):
    combine_parts(coefs, (c0, c1, c2, c3), mine, sent)


def edge_kernel(me, mine, other, sent):
    for parity, outer, facing in ((0, 0, 0), (1, 8, 8)):
        @pl.when(me[1] == parity)
        def _(outer=outer, facing=facing):
            for z in range(ZD):
                sent[z] = (mine[4 + z] + other[facing + z].astype(F32)).astype(BF16)
                sent[ZD + z] = mine[outer + z].astype(BF16)


def pieces_body(me, coefs, mine, other, outer, inner, g_out, outs, begin, note, end):
    def get(ref, z, cut):
        return ref[z, :, cut].astype(F32)

    def even_cells(cut):
        below = [mine[z, :, cut] + get(outer, z, cut) for z in range(ZD)]
        own = [mine[4 + z, :, cut] + get(other, z, cut) + get(outer, 4 + z, cut) for z in range(ZD)]
        above = [mine[8 + z, :, cut] + get(other, 4 + z, cut) + get(inner, 4 + z, cut) for z in range(ZD)]
        return below, own, above

    def odd_cells(cut):
        below = [mine[z, :, cut] + get(other, 4 + z, cut) + get(inner, 4 + z, cut) for z in range(ZD)]
        own = [mine[4 + z, :, cut] + get(other, 8 + z, cut) + get(outer, 4 + z, cut) for z in range(ZD)]
        above = [mine[8 + z, :, cut] + get(outer, z, cut) for z in range(ZD)]
        return below, own, above

    for parity, cells_of in ((0, even_cells), (1, odd_cells)):
        @pl.when(me[1] == parity)
        def _(cells_of=cells_of):
            kept = begin()
            for cut in cuts():
                below, own, above = cells_of(cut)
                for z in range(ZD):
                    g_out[z, :, cut] = own[z]
                    kept = note(kept, z, cut, own[z])
                cells = below + own + above
                for r in range(ANG):
                    for i in range(PAIR):
                        total = None
                        for e in range(12):
                            term = coefs[r, i, e:e + 1, :] * cells[e]
                            total = term if total is None else total + term
                        outs[r][i, :, cut] = total.astype(outs[r].dtype)
            end(kept)


def pieces_first(me, coefs, mine, other, outer, inner, g_out, h0, h1, h2, h3, dots):
    def note(kept, z, cut, value):
        return kept + fold(value * value)

    def end(kept):
        dots[...] = kept

    pieces_body(me, coefs, mine, other, outer, inner, g_out, (h0, h1, h2, h3),
                lambda: jnp.zeros((8, 128), F32), note, end)


def pieces_second(me, coefs, g0, mine, other, outer, inner, g_out, h0, h1, h2, h3, dots):
    def note(kept, z, cut, value):
        return kept[0] + fold(value * g0[z, :, cut]), kept[1] + fold(value * value)

    def end(kept):
        dots[:8] = kept[0]
        dots[8:] = kept[1]

    pieces_body(me, coefs, mine, other, outer, inner, g_out, (h0, h1, h2, h3),
                lambda: (jnp.zeros((8, 128), F32),) * 2, note, end)


def last_kernel(me, coefs, c0, c1, c2, c3, own, inner, outer):
    for parity, far, near in ((0, 0, 8), (1, 8, 0)):
        @pl.when(me[1] == parity)
        def _(far=far, near=near):
            for cut in cuts():
                totals = spread_slices(coefs, (c0, c1, c2, c3), cut)
                for z in range(ZD):
                    outer[z, :, cut] = totals[far + z]
                    own[z, :, cut] = totals[4 + z]
                    inner[z, :, cut] = totals[near + z]


def steps(sums_ref):
    total = sums_ref[0]
    for at in range(1, sums_ref.shape[0]):
        total = total + sums_ref[at]
    lane = lax.broadcasted_iota(jnp.int32, (1, 128), 1)
    gamma0, curve0, inner, norm, cross, own = [
        jnp.sum(jnp.where(lane == at, total, 0.0)) for at in range(6)
    ]
    step0 = gamma0 / curve0
    gamma1 = gamma0 - 2.0 * step0 * inner + step0 * step0 * norm
    ratio = gamma1 / gamma0
    curve1 = (1.0 + ratio) * (1.0 + ratio) * curve0 - 2.0 * (1.0 + ratio) * step0 * cross + step0 * step0 * own
    step1 = gamma1 / curve1
    return step0 + step1 * (1.0 + ratio), step0 * step1


def volume_kernel(sums, g0, z0, out):
    one, two = steps(sums)
    for z in range(ZD):
        out[z] = (one * g0[z] - two * z0[z]).astype(BF16)


def gradient_kernel(sums, t1, inner, outer, g0, z0, out):
    one, two = steps(sums)
    for z in range(ZD):
        last = t1[z] + inner[z] + outer[z]
        out[z] = (g0[z] - one * z0[z] + two * last).astype(BF16)


def residual_kernel(sums, p, q0, w0, out):
    one, two = steps(sums)
    for a in range(PAIR):
        out[a, 0] = p[a, 0] - one * q0[a] + two * w0[a]


def place_kernel(me_ref, s0, s1, s2, s3, out):
    def place(at, share):
        out[:, :, at] = share[...].astype(F32)

    gather_shares(me_ref[0], (s0, s1, s2, s3), place)


def along_ang(value, other):
    return lax.ppermute(value, "ang", [(i, i ^ other) for i in range(ANG)])


def on_chip(value):
    return lax.ppermute(value, "slab", [(i, i ^ 1) for i in range(lax.axis_size("slab"))])


def across(value):
    count = lax.axis_size("slab")
    return lax.ppermute(
        value, "slab", [pair for i in range(1, count - 1, 2) for pair in ((i, i + 1), (i + 1, i))]
    )


def exchange(shares):
    far = along_ang(shares[2], 2)
    near = along_ang(shares[1], 1)
    back = along_ang(shares[3], 3)
    return (shares[0], near, far, back)


def per_device(projections, weights, columns, row_weights, reach):
    me = jnp.stack([lax.axis_index("ang"), lax.axis_index("slab") % 2]).astype(jnp.int32)
    row = sds((PAIR * ZD, 128), F32)
    inner, outer = call(mask_kernel, [row] * 2, [SMEM] * 3)(me, row_weights, reach)
    outer = across(outer)
    edges = (on_chip(inner), outer)

    cols = columns.transpose(2, 0, 1)

    def share(dtype, more=0):
        return sds((PAIR, L, Q + more), dtype)

    full = sds((PAIR, L, X), F32)
    part = sds((ZD, L, Q), F32)
    part_b = sds((ZD, L, Q), BF16)
    acc = pltpu.VMEM((PAIR, L, X), F32)
    macs = 2 * PAIR * L * UB * 384 * 128
    sent = [sds((3 * ZD, L, Q), F32), sds((3 * ZD, L, Q), BF16)]

    def halo(mine, sent):
        other = on_chip(sent)
        (edge,) = call(edge_kernel, [sds((2 * ZD, L, Q), BF16)], [SMEM] + [VMEM] * 2)(me, mine, other)
        outer = across(edge)
        return mine, other, outer, on_chip(outer)

    *shares, w = call(
        back_kernel, [share(BF16, COEF)] * 4 + [sds((PAIR, UB, 384, 128), BF16)],
        [SMEM] * 3 + [VMEM] * 3 + [HBM], [acc, pltpu.SemaphoreType.DMA((PAIR, UB // GROUP))],
        flops=2 * macs, nbytes=7_000_000, limit=46,
    )(me, cols, row_weights, *edges, projections, weights.reshape(PAIR, UB, 384, 128))
    *spread, coefs = call(
        open_kernel, sent + [sds((ANG, PAIR, L, 128), F32)], [VMEM] * 4, flops=10_000_000
    )(*exchange(shares))
    g0, *shares, gamma = call(
        pieces_first, [part] + [share(BF16)] * 4 + [sds((8, 128), F32)], [SMEM] + [VMEM] * 5, flops=10_000_000
    )(me, coefs, *halo(*spread))

    *shares, q0, curve = call(
        first_kernel, [share(MID)] * 4 + [full, sds((8, 128), F32)],
        [SMEM] * 2 + [VMEM] * 5, [pltpu.VMEM((PAIR, L, X), BF16), acc],
        flops=3 * macs, nbytes=7_000_000,
    )(me, cols, *exchange(shares), w)
    spread = call(combine_kernel, sent, [VMEM] * 5, flops=10_000_000)(coefs, *exchange(shares))
    z0, *shares, inner = call(
        pieces_second, [part] + [share(F32)] * 4 + [sds((16, 128), F32)], [SMEM] + [VMEM] * 6, flops=10_000_000
    )(me, coefs, g0, *halo(*spread))

    *shares, w0, sums = call(
        second_kernel, [share(F32)] * 4 + [full, sds((lax.axis_size("slab") * ANG, 1, 128), F32)],
        [SMEM] * 2 + [VMEM] * 9, [pltpu.VMEM((PAIR, 2 * L, X), BF16), acc],
        flops=4 * macs, nbytes=9_000_000,
    )(me, cols, *exchange(shares), q0, gamma, curve, inner, w)
    shares = exchange(shares)
    sums = lax.all_to_all(sums, ("slab", "ang"), 0, 0, tiled=True)
    (volume,) = call(volume_kernel, [part_b], [VMEM] * 3)(sums, g0, z0)
    (residual,) = call(residual_kernel, [sds(projections.shape, F32)], [VMEM] * 4)(sums, projections, q0, w0)
    volume = exchange((volume,) * 4)
    t1, inner, outer = call(last_kernel, [part] * 3, [SMEM] + [VMEM] * 5, flops=10_000_000)(me, coefs, *shares)
    outer = across(outer)
    (gradient,) = call(gradient_kernel, [part_b], [VMEM] * 6)(sums, t1, on_chip(inner), outer, g0, z0)
    whole = [sds((ZD, L, X), F32)]
    (volume,) = call(place_kernel, whole, [SMEM] + [VMEM] * 4)(me, *volume)
    (gradient,) = call(place_kernel, whole, [SMEM] + [VMEM] * 4)(me, *exchange((gradient,) * 4))
    return volume, residual, gradient


def solution(mesh):
    in_specs = (
        P("ang", "slab", None, None),
        P("ang", None, None, None, None),
        P("ang", None, None),
        P("ang", "slab", None, None, None),
        P("ang", "slab", None),
    )
    out_specs = (P("slab", None, None), P("ang", "slab", None, None), P("slab", None, None))
    return jax.shard_map(
        per_device, mesh=mesh, in_specs=in_specs, out_specs=out_specs, check_vma=False
    )
```

```python
import functools

import jax
import jax.numpy as jnp
from jax import lax
from jax.experimental import pallas as pl
from jax.experimental.pallas import tpu as pltpu
from jax.sharding import PartitionSpec as P

F32 = jnp.float32
BF16 = jnp.bfloat16
ANG = 4
PAIR = 2
L = 16
X = 4096
Q = X // ANG
UB = 32
ZD = 4
AHEAD = 3
CH = 128
COEF = 3 * 128
GROUP = 8
VMEM = pl.BlockSpec(memory_space=pltpu.VMEM)
SMEM = pl.BlockSpec(memory_space=pltpu.SMEM)
MID = BF16
HBM = pl.BlockSpec(memory_space=pltpu.HBM)


def call(kernel, outs, specs, scratch=(), flops=0, nbytes=2_000_000, limit=24):
    return pl.pallas_call(
        kernel,
        out_shape=outs,
        in_specs=specs,
        out_specs=[VMEM] * len(outs),
        scratch_shapes=list(scratch),
        compiler_params=pltpu.CompilerParams(vmem_limit_bytes=limit * 1024 * 1024),
        cost_estimate=pl.CostEstimate(flops=flops, bytes_accessed=nbytes, transcendentals=0),
    )


def sds(shape, dtype):
    return jax.ShapeDtypeStruct(shape, dtype)


def halves(value):
    high = value.astype(BF16)
    low = (value - high.astype(F32)).astype(BF16)
    return jnp.concatenate([high, low], axis=0)


def fold(value):
    total = value[:8] + value[8:]
    out = total[:, :128]
    for at in range(1, total.shape[1] // 128):
        out = out + total[:, 128 * at:128 * (at + 1)]
    return out


def window(cols, a, block):
    return pl.ds(pl.multiple_of(cols[0, a, block] * 128, 128), 384)


def back_block(a, block, value, cols, w, acc):
    both = halves(value)
    spread = lax.dot_general(
        both, w[a, block], (((1,), (1,)), ((), ())), preferred_element_type=F32
    )
    at = window(cols, a, block)
    acc[a, :, at] += spread[:L] + spread[L:]


def send_shares(me, acc, outs):
    for r in range(ANG):
        quarter = me ^ r
        share = acc[:, :, pl.ds(pl.multiple_of(quarter * Q, Q), Q)]
        outs[r][:, :, :Q] = share.astype(outs[r].dtype)


def open_inputs(me, rows_hbm, reach_hbm, cols_hbm, p_hbm, inner, own, outer, cols, p, rows, reach, sem):
    copies = [
        pltpu.make_async_copy(src, dst, sem.at[at])
        for at, (src, dst) in enumerate(((rows_hbm, rows), (reach_hbm, reach), (cols_hbm, cols), (p_hbm, p)))
    ]
    for copy in copies:
        copy.start()
    copies[0].wait()
    copies[1].wait()
    even = me[1] == 0
    for i in range(PAIR):
        for z in range(ZD):
            top = jnp.where(reach[i, 0, 1] == 1, rows[i, 0, 2, 0, z], 0.0)
            low = jnp.where(reach[i, 0, 0] == -1, rows[i, 0, 0, 0, z], 0.0)
            at = slice(ZD * i + z, ZD * i + z + 1)
            inner[at] = jnp.full((1, 128), jnp.where(even, top, low), F32)
            outer[at] = jnp.full((1, 128), jnp.where(even, low, top), F32)
            own[at] = jnp.full((1, 128), rows[i, 0, 1, 0, z], F32)
    copies[2].wait()
    copies[3].wait()


def back_kernel(me_ref, cols, own, inner, outer, p_ref, w_hbm, o0, o1, o2, o3, w, acc, sem):
    copies = []
    for a in range(PAIR):
        for g in range(UB // GROUP):
            span = pl.ds(GROUP * g, GROUP)
            copies.append(pltpu.make_async_copy(w_hbm.at[a, span], w.at[a, span], sem.at[a, g]))
    for copy in copies[:AHEAD]:
        copy.start()
    acc[...] = jnp.zeros_like(acc)
    for a in range(PAIR):
        for block in range(UB):
            at = (a * UB + block) // GROUP
            if block % GROUP == 0:
                copies[at].wait()
                if at + AHEAD < len(copies):
                    copies[at + AHEAD].start()
            back_block(a, block, p_ref[a, 0, :, 128 * block:128 * (block + 1)], cols, w, acc)
    outs = (o0, o1, o2, o3)
    send_shares(me_ref[0], acc, outs)
    even = me_ref[1] == 0
    from_low = jnp.where(even, outer[...], inner[...])
    from_high = jnp.where(even, inner[...], outer[...])
    for i in range(PAIR):
        at = slice(ZD * i, ZD * (i + 1))
        rest = jnp.concatenate([from_low[at], own[at], from_high[at], jnp.zeros((4, 128), F32)], axis=0)
        for part in range(3):
            piece = rest.astype(BF16)
            rest = rest - piece.astype(F32)
            for out in outs:
                out[i, :, Q + 128 * part:Q + 128 * (part + 1)] = piece


def both_body(cols, w, acc, lhs, store):
    acc[...] = jnp.zeros_like(acc)
    for a in range(PAIR):
        for g in range(UB // GROUP):
            images = []
            for i in range(GROUP):
                block = g * GROUP + i
                image = jnp.dot(lhs(a, window(cols, a, block)), w[a, block], preferred_element_type=F32)
                if image.shape[0] > L:
                    image = image[:L] + image[L:]
                store(a, block, image)
                images.append(image)
            for i in range(GROUP):
                back_block(a, g * GROUP + i, images[i], cols, w, acc)


def gather_shares(me, shares, place):
    for r in range(ANG):
        quarter = me ^ r
        place(pl.ds(pl.multiple_of(quarter * Q, Q), Q), shares[r])


def first_kernel(me_ref, cols, h0, h1, h2, h3, w, o0, o1, o2, o3, q_out, dots, hb, acc):

    def place(at, share):
        hb[:, :, at] = share[...]

    def store(a, block, image):
        q_out[a, :, 128 * block:128 * (block + 1)] = image

    gather_shares(me_ref[0], (h0, h1, h2, h3), place)
    both_body(cols, w, acc, lambda a, at: hb[a, :, at], store)
    send_shares(me_ref[0], acc, (o0, o1, o2, o3))
    dots[...] = fold(q_out[0] * q_out[0]) + fold(q_out[1] * q_out[1])


def second_kernel(me_ref, cols, h0, h1, h2, h3, q0_ref, gamma_ref, curve_ref, inner_ref, w,
                  o0, o1, o2, o3, w_out, hb, acc):

    def place(at, share):
        hb[:, :, at] = share[...]

    def store(a, block, image):
        w_out[a, :, 128 * block:128 * (block + 1)] = image

    gather_shares(me_ref[0], (h0, h1, h2, h3), place)
    both_body(cols, w, acc, lambda a, at: hb[a, :, at], store)
    send_shares(me_ref[0], acc, (o0, o1, o2, o3))
    cross = fold(w_out[0] * q0_ref[0]) + fold(w_out[1] * q0_ref[1])
    own = fold(w_out[0] * w_out[0]) + fold(w_out[1] * w_out[1])
    lane = lax.broadcasted_iota(jnp.int32, (1, 128), 1)
    row = jnp.zeros((1, 128), F32)
    for at, value in enumerate((gamma_ref[...], curve_ref[...], inner_ref[:8], inner_ref[8:], cross, own)):
        row = jnp.where(lane == at, jnp.sum(value), row)
    for out in (o0, o1, o2, o3):
        out[:, :, Q:] = jnp.broadcast_to(row[None], (PAIR, L, 128))


def spread_slices(coefs, parts, cut):
    totals = [None] * 12
    for r in range(ANG):
        for i in range(PAIR):
            value = parts[r][i, :, cut].astype(F32)
            for e in range(12):
                term = coefs[r, i, e:e + 1, :] * value
                totals[e] = term if totals[e] is None else totals[e] + term
    return totals


def cuts():
    return [pl.ds(at * CH, CH) for at in range(Q // CH)]


def combine_parts(coefs, parts, mine, sent):
    for cut in cuts():
        for e, total in enumerate(spread_slices(coefs, parts, cut)):
            mine[e, :, cut] = total
            sent[e, :, cut] = total.astype(BF16)


def open_kernel(c0, c1, c2, c3, mine, sent, coefs):
    parts = (c0, c1, c2, c3)
    for r in range(ANG):
        for i in range(PAIR):
            value = parts[r][i, :, Q:Q + 128].astype(F32)
            value = value + parts[r][i, :, Q + 128:Q + 256].astype(F32)
            coefs[r, i] = value + parts[r][i, :, Q + 256:].astype(F32)
    combine_parts(coefs, parts, mine, sent)


def combine_kernel(coefs, c0, c1, c2, c3, mine, sent):
    combine_parts(coefs, (c0, c1, c2, c3), mine, sent)


def edge_kernel(me, mine, other, sent):
    for parity, outer, facing in ((0, 0, 0), (1, 8, 8)):
        @pl.when(me[1] == parity)
        def _(outer=outer, facing=facing):
            for z in range(ZD):
                sent[z] = (mine[4 + z] + other[facing + z].astype(F32)).astype(BF16)
                sent[ZD + z] = mine[outer + z].astype(BF16)


def pieces_body(me, coefs, mine, other, outer, inner, g_out, outs, begin, note, end):
    def get(ref, z, cut):
        return ref[z, :, cut].astype(F32)

    def even_cells(cut):
        below = [mine[z, :, cut] + get(outer, z, cut) for z in range(ZD)]
        own = [mine[4 + z, :, cut] + get(other, z, cut) + get(outer, 4 + z, cut) for z in range(ZD)]
        above = [mine[8 + z, :, cut] + get(other, 4 + z, cut) + get(inner, 4 + z, cut) for z in range(ZD)]
        return below, own, above

    def odd_cells(cut):
        below = [mine[z, :, cut] + get(other, 4 + z, cut) + get(inner, 4 + z, cut) for z in range(ZD)]
        own = [mine[4 + z, :, cut] + get(other, 8 + z, cut) + get(outer, 4 + z, cut) for z in range(ZD)]
        above = [mine[8 + z, :, cut] + get(outer, z, cut) for z in range(ZD)]
        return below, own, above

    for parity, cells_of in ((0, even_cells), (1, odd_cells)):
        @pl.when(me[1] == parity)
        def _(cells_of=cells_of):
            kept = begin()
            for cut in cuts():
                below, own, above = cells_of(cut)
                for z in range(ZD):
                    g_out[z, :, cut] = own[z]
                    kept = note(kept, z, cut, own[z])
                cells = below + own + above
                for r in range(ANG):
                    for i in range(PAIR):
                        total = None
                        for e in range(12):
                            term = coefs[r, i, e:e + 1, :] * cells[e]
                            total = term if total is None else total + term
                        outs[r][i, :, cut] = total.astype(outs[r].dtype)
            end(kept)


def pieces_first(me, coefs, mine, other, outer, inner, g_out, h0, h1, h2, h3, dots):
    def note(kept, z, cut, value):
        return kept + fold(value * value)

    def end(kept):
        dots[...] = kept

    pieces_body(me, coefs, mine, other, outer, inner, g_out, (h0, h1, h2, h3),
                lambda: jnp.zeros((8, 128), F32), note, end)


def pieces_second(me, coefs, g0, mine, other, outer, inner, g_out, h0, h1, h2, h3, dots):
    def note(kept, z, cut, value):
        return kept[0] + fold(value * g0[z, :, cut]), kept[1] + fold(value * value)

    def end(kept):
        dots[:8] = kept[0]
        dots[8:] = kept[1]

    pieces_body(me, coefs, mine, other, outer, inner, g_out, (h0, h1, h2, h3),
                lambda: (jnp.zeros((8, 128), F32),) * 2, note, end)


def last_kernel(me, coefs, c0, c1, c2, c3, own, inner, outer, sums):
    row = (c0[0, :1, Q:] + c1[0, :1, Q:]) + (c2[0, :1, Q:] + c3[0, :1, Q:])
    sums[...] = jnp.broadcast_to(row[None], sums.shape)
    for parity, far, near in ((0, 0, 8), (1, 8, 0)):
        @pl.when(me[1] == parity)
        def _(far=far, near=near):
            for cut in cuts():
                totals = spread_slices(coefs, (c0, c1, c2, c3), cut)
                for z in range(ZD):
                    outer[z, :, cut] = totals[far + z]
                    own[z, :, cut] = totals[4 + z]
                    inner[z, :, cut] = totals[near + z]


def steps(sums_ref):
    total = sums_ref[0]
    for at in range(1, sums_ref.shape[0]):
        total = total + sums_ref[at]
    lane = lax.broadcasted_iota(jnp.int32, (1, 128), 1)
    gamma0, curve0, inner, norm, cross, own = [
        jnp.sum(jnp.where(lane == at, total, 0.0)) for at in range(6)
    ]
    step0 = gamma0 / curve0
    gamma1 = gamma0 - 2.0 * step0 * inner + step0 * step0 * norm
    ratio = gamma1 / gamma0
    curve1 = (1.0 + ratio) * (1.0 + ratio) * curve0 - 2.0 * (1.0 + ratio) * step0 * cross + step0 * step0 * own
    step1 = gamma1 / curve1
    return step0 + step1 * (1.0 + ratio), step0 * step1


def volume_kernel(sums, g0, z0, out):
    one, two = steps(sums)
    for z in range(ZD):
        out[z] = (one * g0[z] - two * z0[z]).astype(BF16)


def gradient_kernel(sums, t1, inner, outer, g0, z0, out):
    one, two = steps(sums)
    for z in range(ZD):
        last = t1[z] + inner[z] + outer[z]
        out[z] = (g0[z] - one * z0[z] + two * last).astype(BF16)


def residual_kernel(sums, p, q0, w0, out):
    one, two = steps(sums)
    for a in range(PAIR):
        out[a, 0] = p[a, 0] - one * q0[a] + two * w0[a]


def place_kernel(me_ref, s0, s1, s2, s3, out):
    def place(at, share):
        out[:, :, at] = share[...].astype(F32)

    gather_shares(me_ref[0], (s0, s1, s2, s3), place)


def along_ang(value, other):
    return lax.ppermute(value, "ang", [(i, i ^ other) for i in range(ANG)])


def on_chip(value):
    return lax.ppermute(value, "slab", [(i, i ^ 1) for i in range(lax.axis_size("slab"))])


def across(value):
    count = lax.axis_size("slab")
    return lax.ppermute(
        value, "slab", [pair for i in range(1, count - 1, 2) for pair in ((i, i + 1), (i + 1, i))]
    )


def exchange(shares):
    far = along_ang(shares[2], 2)
    near = along_ang(shares[1], 1)
    back = along_ang(shares[3], 3)
    return (shares[0], near, far, back)


def per_device(projections, weights, columns, row_weights, reach):
    me = jnp.stack([lax.axis_index("ang"), lax.axis_index("slab") % 2]).astype(jnp.int32)
    row = sds((PAIR * ZD, 128), F32)
    inner, own, outer, cols, p = call(
        open_inputs, [row] * 3 + [sds((3, PAIR, UB), jnp.int32), sds(projections.shape, F32)], [SMEM] + [HBM] * 4,
        [pltpu.SMEM(row_weights.shape, F32), pltpu.SMEM(reach.shape, jnp.int32), pltpu.SemaphoreType.DMA((4,))],
        limit=53,
    )(me, row_weights, reach, columns.transpose(2, 0, 1), projections)
    outer = across(outer)
    edges = (own, on_chip(inner), outer)

    def share(dtype, more=0):
        return sds((PAIR, L, Q + more), dtype)

    full = sds((PAIR, L, X), F32)
    part = sds((ZD, L, Q), F32)
    part_b = sds((ZD, L, Q), BF16)
    acc = pltpu.VMEM((PAIR, L, X), F32)
    macs = 2 * PAIR * L * UB * 384 * 128
    sent = [sds((3 * ZD, L, Q), F32), sds((3 * ZD, L, Q), BF16)]

    def halo(mine, sent):
        other = on_chip(sent)
        (edge,) = call(edge_kernel, [sds((2 * ZD, L, Q), BF16)], [SMEM] + [VMEM] * 2)(me, mine, other)
        outer = across(edge)
        return mine, other, outer, on_chip(outer)

    *shares, w = call(
        back_kernel, [share(BF16, COEF)] * 4 + [sds((PAIR, UB, 384, 128), BF16)],
        [SMEM] * 2 + [VMEM] * 4 + [HBM], [acc, pltpu.SemaphoreType.DMA((PAIR, UB // GROUP))],
        flops=2 * macs, nbytes=7_000_000, limit=46,
    )(me, cols, *edges, p, weights.reshape(PAIR, UB, 384, 128))
    *spread, coefs = call(
        open_kernel, sent + [sds((ANG, PAIR, L, 128), F32)], [VMEM] * 4, flops=10_000_000
    )(*exchange(shares))
    g0, *shares, gamma = call(
        pieces_first, [part] + [share(BF16)] * 4 + [sds((8, 128), F32)], [SMEM] + [VMEM] * 5, flops=10_000_000
    )(me, coefs, *halo(*spread))

    *shares, q0, curve = call(
        first_kernel, [share(MID)] * 4 + [full, sds((8, 128), F32)],
        [SMEM] * 2 + [VMEM] * 5, [pltpu.VMEM((PAIR, L, X), BF16), acc],
        flops=3 * macs, nbytes=7_000_000,
    )(me, cols, *exchange(shares), w)
    spread = call(combine_kernel, sent, [VMEM] * 5, flops=10_000_000)(coefs, *exchange(shares))
    z0, *shares, inner = call(
        pieces_second, [part] + [share(BF16)] * 4 + [sds((16, 128), F32)], [SMEM] + [VMEM] * 6, flops=10_000_000
    )(me, coefs, g0, *halo(*spread))

    *shares, w0 = call(
        second_kernel, [share(F32, 128)] * 4 + [full],
        [SMEM] * 2 + [VMEM] * 9, [pltpu.VMEM((PAIR, L, X), BF16), acc],
        flops=4 * macs, nbytes=9_000_000,
    )(me, cols, *exchange(shares), q0, gamma, curve, inner, w)
    own, inner, outer, sums = call(
        last_kernel, [part] * 3 + [sds((lax.axis_size("slab"), 1, 128), F32)], [SMEM] + [VMEM] * 5, flops=10_000_000
    )(me, coefs, *exchange(shares))
    outer = across(outer)
    inner = on_chip(inner)
    sums = lax.all_to_all(sums, "slab", 0, 0, tiled=True)
    (volume,) = call(volume_kernel, [part_b], [VMEM] * 3)(sums, g0, z0)
    (residual,) = call(residual_kernel, [sds(projections.shape, F32)], [VMEM] * 4)(sums, projections, q0, w0)
    volume = exchange((volume,) * 4)
    (gradient,) = call(gradient_kernel, [part_b], [VMEM] * 6)(sums, own, inner, outer, g0, z0)
    whole = [sds((ZD, L, X), F32)]
    (volume,) = call(place_kernel, whole, [SMEM] + [VMEM] * 4)(me, *volume)
    (gradient,) = call(place_kernel, whole, [SMEM] + [VMEM] * 4)(me, *exchange((gradient,) * 4))
    return volume, residual, gradient


def solution(mesh):
    in_specs = (
        P("ang", "slab", None, None),
        P("ang", None, None, None, None),
        P("ang", None, None),
        P("ang", "slab", None, None, None),
        P("ang", "slab", None),
    )
    out_specs = (P("slab", None, None), P("ang", "slab", None, None), P("slab", None, None))
    return jax.shard_map(
        per_device, mesh=mesh, in_specs=in_specs, out_specs=out_specs, check_vma=False
    )
```

```python
import functools

import jax
import jax.numpy as jnp
from jax import lax
from jax.experimental import pallas as pl
from jax.experimental.pallas import tpu as pltpu
from jax.sharding import PartitionSpec as P

F32 = jnp.float32
BF16 = jnp.bfloat16
ANG = 4
ORDER = (0, 2, 3, 1)
PAIR = 2
L = 16
X = 4096
Q = X // ANG
UB = 32
ZD = 4
CH = 128
COEF = 3 * 128
CHUNK = 16
GROUP = 8
VMEM = pl.BlockSpec(memory_space=pltpu.VMEM)
SMEM = pl.BlockSpec(memory_space=pltpu.SMEM)
MID = BF16
HBM = pl.BlockSpec(memory_space=pltpu.HBM)


def call(kernel, outs, specs, scratch=(), flops=0, nbytes=2_000_000, limit=24):
    return pl.pallas_call(
        kernel,
        out_shape=outs,
        in_specs=specs,
        out_specs=[VMEM] * len(outs),
        scratch_shapes=list(scratch),
        compiler_params=pltpu.CompilerParams(vmem_limit_bytes=limit * 1024 * 1024),
        cost_estimate=pl.CostEstimate(flops=flops, bytes_accessed=nbytes, transcendentals=0),
    )


def sds(shape, dtype):
    return jax.ShapeDtypeStruct(shape, dtype)


def halves(value):
    high = value.astype(BF16)
    low = (value - high.astype(F32)).astype(BF16)
    return jnp.concatenate([high, low], axis=0)


def fold(value):
    total = value[:8] + value[8:]
    out = total[:, :128]
    for at in range(1, total.shape[1] // 128):
        out = out + total[:, 128 * at:128 * (at + 1)]
    return out


def window(cols, a, block):
    return pl.ds(pl.multiple_of(cols[0, a, block] * 128, 128), 384)


def back_block(a, block, value, cols, w, acc):
    both = halves(value)
    spread = lax.dot_general(
        both, w[a, block], (((1,), (1,)), ((), ())), preferred_element_type=F32
    )
    at = window(cols, a, block)
    acc[a, :, at] += spread[:L] + spread[L:]


def send_shares(me, acc, outs):
    for r in range(ANG):
        quarter = me ^ ORDER[r]
        share = acc[:, :, pl.ds(pl.multiple_of(quarter * Q, Q), Q)]
        outs[r][:, :, :Q] = share.astype(outs[r].dtype)


def open_inputs(parity, rows_hbm, reach_hbm, cols_hbm, p_hbm, inner, own, outer, flag, cols, p, rows, reach, sem):
    copies = [
        pltpu.make_async_copy(src, dst, sem.at[at])
        for at, (src, dst) in enumerate(((rows_hbm, rows), (reach_hbm, reach), (cols_hbm, cols), (p_hbm, p)))
    ]
    for copy in copies:
        copy.start()
    copies[0].wait()
    copies[1].wait()
    flag[...] = jnp.full((L, 128), parity[0], jnp.int32)
    even = parity[0] == 0
    for i in range(PAIR):
        for z in range(ZD):
            top = jnp.where(reach[i, 0, 1] == 1, rows[i, 0, 2, 0, z], 0.0)
            low = jnp.where(reach[i, 0, 0] == -1, rows[i, 0, 0, 0, z], 0.0)
            at = slice(ZD * i + z, ZD * i + z + 1)
            inner[at] = jnp.full((1, 128), jnp.where(even, top, low), F32)
            outer[at] = jnp.full((1, 128), jnp.where(even, low, top), F32)
            own[at] = jnp.full((1, 128), rows[i, 0, 1, 0, z], F32)
    copies[2].wait()
    copies[3].wait()


def back_kernel(me_ref, cols, flag, own, inner, outer, p_ref, w_hbm, o0, o1, o2, o3, w, acc, sem):
    copies = []
    for a in range(PAIR):
        for g in range(UB // CHUNK):
            span = pl.ds(CHUNK * g, CHUNK)
            copies.append(pltpu.make_async_copy(w_hbm.at[a, span], w.at[a, span], sem.at[a, g]))
            copies[-1].start()
    acc[...] = jnp.zeros_like(acc)
    for a in range(PAIR):
        for block in range(UB):
            if block % CHUNK == 0:
                copies[(a * UB + block) // CHUNK].wait()
            back_block(a, block, p_ref[a, 0, :, 128 * block:128 * (block + 1)], cols, w, acc)
    outs = (o0, o1, o2, o3)
    send_shares(me_ref[0], acc, outs)
    even = flag[:8] == 0
    from_low = jnp.where(even, outer[...], inner[...])
    from_high = jnp.where(even, inner[...], outer[...])
    for i in range(PAIR):
        at = slice(ZD * i, ZD * (i + 1))
        rest = jnp.concatenate([from_low[at], own[at], from_high[at], jnp.zeros((4, 128), F32)], axis=0)
        for part in range(3):
            piece = rest.astype(BF16)
            rest = rest - piece.astype(F32)
            for out in outs:
                out[i, :, Q + 128 * part:Q + 128 * (part + 1)] = piece


def both_body(cols, w, acc, lhs, store):
    acc[...] = jnp.zeros_like(acc)
    for a in range(PAIR):
        for g in range(UB // GROUP):
            images = []
            for i in range(GROUP):
                block = g * GROUP + i
                image = jnp.dot(lhs(a, window(cols, a, block)), w[a, block], preferred_element_type=F32)
                if image.shape[0] > L:
                    image = image[:L] + image[L:]
                store(a, block, image)
                images.append(image)
            for i in range(GROUP):
                back_block(a, g * GROUP + i, images[i], cols, w, acc)


def gather_shares(me, shares, place):
    for r in range(ANG):
        quarter = me ^ ORDER[r]
        place(pl.ds(pl.multiple_of(quarter * Q, Q), Q), shares[r])


def first_kernel(me_ref, cols, h0, h1, h2, h3, w, o0, o1, o2, o3, q_out, dots, hb, acc):

    def place(at, share):
        hb[:, :, at] = share[...]

    def store(a, block, image):
        q_out[a, :, 128 * block:128 * (block + 1)] = image

    gather_shares(me_ref[0], (h0, h1, h2, h3), place)
    both_body(cols, w, acc, lambda a, at: hb[a, :, at], store)
    send_shares(me_ref[0], acc, (o0, o1, o2, o3))
    dots[...] = fold(q_out[0] * q_out[0]) + fold(q_out[1] * q_out[1])


def second_kernel(me_ref, cols, h0, h1, h2, h3, q0_ref, gamma_ref, curve_ref, inner_ref, w,
                  o0, o1, o2, o3, w_out, sums, hb, acc):

    def place(at, share):
        hb[:, :, at] = share[...]

    def store(a, block, image):
        w_out[a, :, 128 * block:128 * (block + 1)] = image

    gather_shares(me_ref[0], (h0, h1, h2, h3), place)
    both_body(cols, w, acc, lambda a, at: hb[a, :, at], store)
    send_shares(me_ref[0], acc, (o0, o1, o2, o3))
    cross = fold(w_out[0] * q0_ref[0]) + fold(w_out[1] * q0_ref[1])
    own = fold(w_out[0] * w_out[0]) + fold(w_out[1] * w_out[1])
    lane = lax.broadcasted_iota(jnp.int32, (1, 128), 1)
    row = jnp.zeros((1, 128), F32)
    for at, value in enumerate((gamma_ref[...], curve_ref[...], inner_ref[:8], inner_ref[8:], cross, own)):
        row = jnp.where(lane == at, jnp.sum(value), row)
    sums[...] = jnp.broadcast_to(row[None], sums.shape)


def spread_slices(coefs, parts, cut):
    totals = [None] * 12
    for r in range(ANG):
        for i in range(PAIR):
            value = parts[r][i, :, cut].astype(F32)
            for e in range(12):
                term = coefs[r, i, e:e + 1, :] * value
                totals[e] = term if totals[e] is None else totals[e] + term
    return totals


def is_even(flag, columns=CH):
    return jnp.concatenate([flag[...]] * (columns // 128), axis=1) == 0


def cuts():
    return [pl.ds(at * CH, CH) for at in range(Q // CH)]


def combine_parts(flag, coefs, parts, mine, sent):
    even = is_even(flag)
    for cut in cuts():
        totals = spread_slices(coefs, parts, cut)
        for e, total in enumerate(totals):
            mine[e, :, cut] = total
        for z in range(ZD):
            sent[z, :, cut] = totals[4 + z].astype(BF16)
            sent[ZD + z, :, cut] = jnp.where(even, totals[8 + z], totals[z]).astype(BF16)


def open_kernel(flag, c0, c1, c2, c3, mine, sent, coefs):
    parts = (c0, c1, c2, c3)
    for r in range(ANG):
        for i in range(PAIR):
            value = parts[r][i, :, Q:Q + 128].astype(F32)
            value = value + parts[r][i, :, Q + 128:Q + 256].astype(F32)
            coefs[r, i] = value + parts[r][i, :, Q + 256:].astype(F32)
    combine_parts(flag, coefs, parts, mine, sent)


def combine_kernel(flag, coefs, c0, c1, c2, c3, mine, sent):
    combine_parts(flag, coefs, (c0, c1, c2, c3), mine, sent)


def edge_kernel(flag, mine, other, sent):
    even = is_even(flag, Q)
    for z in range(ZD):
        sent[z] = (mine[4 + z] + other[ZD + z].astype(F32)).astype(BF16)
        sent[ZD + z] = jnp.where(even, mine[z], mine[8 + z]).astype(BF16)


def pieces_body(flag, coefs, mine, other, outer, inner, g_out, outs, kept, note):
    even = is_even(flag)
    for cut in cuts():
        def get(ref, z):
            return ref[z, :, cut].astype(F32)

        cells = [None] * 12
        for z in range(ZD):
            beyond = get(outer, z)
            beside = get(other, z) + get(inner, 4 + z)
            cells[z] = mine[z, :, cut] + jnp.where(even, beyond, beside)
            cells[4 + z] = mine[4 + z, :, cut] + get(other, 4 + z) + get(outer, 4 + z)
            cells[8 + z] = mine[8 + z, :, cut] + jnp.where(even, beside, beyond)
            g_out[z, :, cut] = cells[4 + z]
            kept = note(kept, z, cut, cells[4 + z])
        for r in range(ANG):
            for i in range(PAIR):
                total = None
                for e in range(12):
                    term = coefs[r, i, e:e + 1, :] * cells[e]
                    total = term if total is None else total + term
                outs[r][i, :, cut] = total.astype(outs[r].dtype)
    return kept


def pieces_first(flag, coefs, mine, other, outer, inner, g_out, h0, h1, h2, h3, dots):
    def note(kept, z, cut, value):
        return kept + fold(value * value)

    dots[...] = pieces_body(
        flag, coefs, mine, other, outer, inner, g_out, (h0, h1, h2, h3), jnp.zeros((8, 128), F32), note
    )


def pieces_second(flag, coefs, g0, mine, other, outer, inner, g_out, h0, h1, h2, h3, dots):
    def note(kept, z, cut, value):
        return kept[0] + fold(value * g0[z, :, cut]), kept[1] + fold(value * value)

    dots[:8], dots[8:] = pieces_body(
        flag, coefs, mine, other, outer, inner, g_out, (h0, h1, h2, h3), (jnp.zeros((8, 128), F32),) * 2, note
    )


def last_kernel(flag, coefs, c0, c1, c2, c3, own, inner, outer):
    even = is_even(flag)
    for cut in cuts():
        totals = spread_slices(coefs, (c0, c1, c2, c3), cut)
        for z in range(ZD):
            own[z, :, cut] = totals[4 + z]
            inner[z, :, cut] = jnp.where(even, totals[8 + z], totals[z])
            outer[z, :, cut] = jnp.where(even, totals[z], totals[8 + z])


def steps(sums_ref):
    total = sums_ref[0]
    for at in range(1, sums_ref.shape[0]):
        total = total + sums_ref[at]
    lane = lax.broadcasted_iota(jnp.int32, (1, 128), 1)
    gamma0, curve0, inner, norm, cross, own = [
        jnp.sum(jnp.where(lane == at, total, 0.0)) for at in range(6)
    ]
    step0 = gamma0 / curve0
    gamma1 = gamma0 - 2.0 * step0 * inner + step0 * step0 * norm
    ratio = gamma1 / gamma0
    curve1 = (1.0 + ratio) * (1.0 + ratio) * curve0 - 2.0 * (1.0 + ratio) * step0 * cross + step0 * step0 * own
    step1 = gamma1 / curve1
    return step0 + step1 * (1.0 + ratio), step0 * step1


def volume_kernel(sums, g0, z0, out):
    one, two = steps(sums)
    for z in range(ZD):
        out[z] = (one * g0[z] - two * z0[z]).astype(BF16)


def gradient_kernel(sums, t1, inner, outer, g0, z0, out):
    one, two = steps(sums)
    for z in range(ZD):
        last = t1[z] + inner[z] + outer[z]
        out[z] = (g0[z] - one * z0[z] + two * last).astype(BF16)


def residual_kernel(sums, p, q0, w0, out):
    one, two = steps(sums)
    for a in range(PAIR):
        out[a, 0] = p[a, 0] - one * q0[a] + two * w0[a]


def place_kernel(me_ref, s0, s1, s2, s3, out):
    def place(at, share):
        out[:, :, at] = share[...].astype(F32)

    gather_shares(me_ref[0], (s0, s1, s2, s3), place)


def along_ang(value, other):
    return lax.ppermute(value, "ang", [(i, i ^ other) for i in range(ANG)])


def on_chip(value):
    return lax.ppermute(value, "slab", [(i, i ^ 1) for i in range(lax.axis_size("slab"))])


def across(value):
    count = lax.axis_size("slab")
    return lax.ppermute(
        value, "slab", [pair for i in range(1, count - 1, 2) for pair in ((i, i + 1), (i + 1, i))]
    )


def exchange(shares):
    return (shares[0],) + tuple(along_ang(shares[i], ORDER[i]) for i in range(1, ANG))


def per_device(projections, weights, columns, row_weights, reach):
    me = lax.axis_index("ang").astype(jnp.int32).reshape(1)
    parity = (lax.axis_index("slab").astype(jnp.int32) & 1).reshape(1)
    row = sds((PAIR * ZD, 128), F32)
    inner, own, outer, flag, cols, p = call(
        open_inputs, [row] * 3 + [sds((L, 128), jnp.int32), sds((3, PAIR, UB), jnp.int32), sds(projections.shape, F32)], [SMEM] + [HBM] * 4,
        [pltpu.SMEM(row_weights.shape, F32), pltpu.SMEM(reach.shape, jnp.int32), pltpu.SemaphoreType.DMA((4,))],
        limit=53,
    )(parity, row_weights, reach, columns.transpose(2, 0, 1), projections)
    outer = across(outer)
    edges = (flag, own, on_chip(inner), outer)

    def share(dtype, more=0):
        return sds((PAIR, L, Q + more), dtype)

    full = sds((PAIR, L, X), F32)
    part = sds((ZD, L, Q), F32)
    part_b = sds((ZD, L, Q), BF16)
    acc = pltpu.VMEM((PAIR, L, X), F32)
    macs = 2 * PAIR * L * UB * 384 * 128
    sent = [sds((3 * ZD, L, Q), F32), sds((2 * ZD, L, Q), BF16)]

    def halo(mine, sent):
        other = on_chip(sent)
        (edge,) = call(edge_kernel, [sds((2 * ZD, L, Q), BF16)], [VMEM] * 3)(flag, mine, other)
        outer = across(edge)
        return mine, other, outer, on_chip(outer)

    *shares, w = call(
        back_kernel, [share(BF16, COEF)] * 4 + [sds((PAIR, UB, 384, 128), BF16)],
        [SMEM] * 2 + [VMEM] * 5 + [HBM], [acc, pltpu.SemaphoreType.DMA((PAIR, UB // CHUNK))],
        flops=2 * macs, nbytes=7_000_000, limit=46,
    )(me, cols, *edges, p, weights.reshape(PAIR, UB, 384, 128))
    *spread, coefs = call(
        open_kernel, sent + [sds((ANG, PAIR, L, 128), F32)], [VMEM] * 5, flops=10_000_000
    )(flag, *exchange(shares))
    g0, *shares, gamma = call(
        pieces_first, [part] + [share(BF16)] * 4 + [sds((8, 128), F32)], [VMEM] * 6, flops=10_000_000
    )(flag, coefs, *halo(*spread))

    *shares, q0, curve = call(
        first_kernel, [share(MID)] * 4 + [full, sds((8, 128), F32)],
        [SMEM] * 2 + [VMEM] * 5, [pltpu.VMEM((PAIR, L, X), BF16), acc],
        flops=3 * macs, nbytes=7_000_000,
    )(me, cols, *exchange(shares), w)
    spread = call(combine_kernel, sent, [VMEM] * 6, flops=10_000_000)(flag, coefs, *exchange(shares))
    z0, *shares, inner = call(
        pieces_second, [part] + [share(BF16)] * 4 + [sds((16, 128), F32)], [VMEM] * 7, flops=10_000_000
    )(flag, coefs, g0, *halo(*spread))

    *shares, w0, sums = call(
        second_kernel, [share(F32)] * 4 + [full, sds((lax.axis_size("slab") * ANG, 1, 128), F32)],
        [SMEM] * 2 + [VMEM] * 9, [pltpu.VMEM((PAIR, L, X), BF16), acc],
        flops=4 * macs, nbytes=9_000_000,
    )(me, cols, *exchange(shares), q0, gamma, curve, inner, w)
    shares = exchange(shares)
    sums = lax.all_to_all(sums, ("slab", "ang"), 0, 0, tiled=True)
    own, inner, outer = call(last_kernel, [part] * 3, [VMEM] * 6, flops=10_000_000)(flag, coefs, *shares)
    outer = across(outer)
    inner = on_chip(inner)
    (volume,) = call(volume_kernel, [part_b], [VMEM] * 3)(sums, g0, z0)
    (residual,) = call(residual_kernel, [sds(projections.shape, F32)], [VMEM] * 4)(sums, projections, q0, w0)
    volume = exchange((volume,) * 4)
    (gradient,) = call(gradient_kernel, [part_b], [VMEM] * 6)(sums, own, inner, outer, g0, z0)
    whole = [sds((ZD, L, X), F32)]
    (volume,) = call(place_kernel, whole, [SMEM] + [VMEM] * 4)(me, *volume)
    (gradient,) = call(place_kernel, whole, [SMEM] + [VMEM] * 4)(me, *exchange((gradient,) * 4))
    return volume, residual, gradient


def solution(mesh):
    in_specs = (
        P("ang", "slab", None, None),
        P("ang", None, None, None, None),
        P("ang", None, None),
        P("ang", "slab", None, None, None),
        P("ang", "slab", None),
    )
    out_specs = (P("slab", None, None), P("ang", "slab", None, None), P("slab", None, None))
    return jax.shard_map(
        per_device, mesh=mesh, in_specs=in_specs, out_specs=out_specs, check_vma=False
    )
```

```python
import functools

import jax
import jax.numpy as jnp
from jax import lax
from jax.experimental import pallas as pl
from jax.experimental.pallas import tpu as pltpu
from jax.sharding import PartitionSpec as P

F32 = jnp.float32
BF16 = jnp.bfloat16
ANG = 4
ORDER = (0, 2, 3, 1)
PAIR = 2
L = 16
X = 4096
Q = X // ANG
UB = 32
ZD = 4
CH = 128
COEF = 3 * 128
CHUNK = 16
GROUP = 8
VMEM = pl.BlockSpec(memory_space=pltpu.VMEM)
SMEM = pl.BlockSpec(memory_space=pltpu.SMEM)
MID = BF16
HBM = pl.BlockSpec(memory_space=pltpu.HBM)


def call(kernel, outs, specs, scratch=(), flops=0, nbytes=2_000_000, limit=24):
    return pl.pallas_call(
        kernel,
        out_shape=outs,
        in_specs=specs,
        out_specs=[VMEM] * len(outs),
        scratch_shapes=list(scratch),
        compiler_params=pltpu.CompilerParams(vmem_limit_bytes=limit * 1024 * 1024),
        cost_estimate=pl.CostEstimate(flops=flops, bytes_accessed=nbytes, transcendentals=0),
    )


def sds(shape, dtype):
    return jax.ShapeDtypeStruct(shape, dtype)


def halves(value):
    high = value.astype(BF16)
    low = (value - high.astype(F32)).astype(BF16)
    return jnp.concatenate([high, low], axis=0)


def fold(value):
    total = value[:8] + value[8:]
    out = total[:, :128]
    for at in range(1, total.shape[1] // 128):
        out = out + total[:, 128 * at:128 * (at + 1)]
    return out


def window(cols, a, block):
    return pl.ds(pl.multiple_of(cols[0, a, block] * 128, 128), 384)


def back_block(a, block, value, cols, w, acc):
    both = halves(value)
    spread = lax.dot_general(
        both, w[a, block], (((1,), (1,)), ((), ())), preferred_element_type=F32
    )
    at = window(cols, a, block)
    acc[a, :, at] += spread[:L] + spread[L:]


def send_shares(me, acc, outs):
    for r in range(ANG):
        quarter = me ^ ORDER[r]
        share = acc[:, :, pl.ds(pl.multiple_of(quarter * Q, Q), Q)]
        outs[r][:, :, :Q] = share.astype(outs[r].dtype)


def open_inputs(parity, rows_hbm, reach_hbm, cols_hbm, p_hbm, inner, own, outer, flag, cols, p, rows, reach, sem):
    copies = [
        pltpu.make_async_copy(src, dst, sem.at[at])
        for at, (src, dst) in enumerate(((rows_hbm, rows), (reach_hbm, reach), (cols_hbm, cols), (p_hbm, p)))
    ]
    for copy in copies:
        copy.start()
    copies[0].wait()
    copies[1].wait()
    flag[...] = jnp.full((L, 128), parity[0], jnp.int32)
    even = parity[0] == 0
    for i in range(PAIR):
        for z in range(ZD):
            top = jnp.where(reach[i, 0, 1] == 1, rows[i, 0, 2, 0, z], 0.0)
            low = jnp.where(reach[i, 0, 0] == -1, rows[i, 0, 0, 0, z], 0.0)
            at = slice(ZD * i + z, ZD * i + z + 1)
            inner[at] = jnp.full((1, 128), jnp.where(even, top, low), F32)
            outer[at] = jnp.full((1, 128), jnp.where(even, low, top), F32)
            own[at] = jnp.full((1, 128), rows[i, 0, 1, 0, z], F32)
    copies[2].wait()
    copies[3].wait()


def back_kernel(me_ref, cols, p_ref, w_hbm, o0, o1, o2, o3, w, acc, sem):
    copies = []
    for a in range(PAIR):
        for g in range(UB // CHUNK):
            span = pl.ds(CHUNK * g, CHUNK)
            copies.append(pltpu.make_async_copy(w_hbm.at[a, span], w.at[a, span], sem.at[a, g]))
            copies[-1].start()
    acc[...] = jnp.zeros_like(acc)
    for a in range(PAIR):
        for block in range(UB):
            if block % CHUNK == 0:
                copies[(a * UB + block) // CHUNK].wait()
            back_block(a, block, p_ref[a, 0, :, 128 * block:128 * (block + 1)], cols, w, acc)
    send_shares(me_ref[0], acc, (o0, o1, o2, o3))


def stencil_kernel(flag, own, inner, outer, c0, c1, c2, c3, o0, o1, o2, o3):
    outs = (o0, o1, o2, o3)
    for share, out in zip((c0, c1, c2, c3), outs):
        out[:, :, :Q] = share[...]
    even = flag[:8] == 0
    from_low = jnp.where(even, outer[...], inner[...])
    from_high = jnp.where(even, inner[...], outer[...])
    for i in range(PAIR):
        at = slice(ZD * i, ZD * (i + 1))
        rest = jnp.concatenate([from_low[at], own[at], from_high[at], jnp.zeros((4, 128), F32)], axis=0)
        for part in range(3):
            piece = rest.astype(BF16)
            rest = rest - piece.astype(F32)
            for out in outs:
                out[i, :, Q + 128 * part:Q + 128 * (part + 1)] = piece


def both_body(cols, w, acc, lhs, store):
    acc[...] = jnp.zeros_like(acc)
    for a in range(PAIR):
        for g in range(UB // GROUP):
            images = []
            for i in range(GROUP):
                block = g * GROUP + i
                image = jnp.dot(lhs(a, window(cols, a, block)), w[a, block], preferred_element_type=F32)
                if image.shape[0] > L:
                    image = image[:L] + image[L:]
                store(a, block, image)
                images.append(image)
            for i in range(GROUP):
                back_block(a, g * GROUP + i, images[i], cols, w, acc)


def gather_shares(me, shares, place):
    for r in range(ANG):
        quarter = me ^ ORDER[r]
        place(pl.ds(pl.multiple_of(quarter * Q, Q), Q), shares[r])


def first_kernel(me_ref, cols, h0, h1, h2, h3, w, o0, o1, o2, o3, q_out, dots, hb, acc):

    def place(at, share):
        hb[:, :, at] = share[...]

    def store(a, block, image):
        q_out[a, :, 128 * block:128 * (block + 1)] = image

    gather_shares(me_ref[0], (h0, h1, h2, h3), place)
    both_body(cols, w, acc, lambda a, at: hb[a, :, at], store)
    send_shares(me_ref[0], acc, (o0, o1, o2, o3))
    dots[...] = fold(q_out[0] * q_out[0]) + fold(q_out[1] * q_out[1])


def second_kernel(me_ref, cols, h0, h1, h2, h3, q0_ref, gamma_ref, curve_ref, inner_ref, w,
                  o0, o1, o2, o3, w_out, sums, hb, acc):

    def place(at, share):
        hb[:, :, at] = share[...]

    def store(a, block, image):
        w_out[a, :, 128 * block:128 * (block + 1)] = image

    gather_shares(me_ref[0], (h0, h1, h2, h3), place)
    both_body(cols, w, acc, lambda a, at: hb[a, :, at], store)
    send_shares(me_ref[0], acc, (o0, o1, o2, o3))
    cross = fold(w_out[0] * q0_ref[0]) + fold(w_out[1] * q0_ref[1])
    own = fold(w_out[0] * w_out[0]) + fold(w_out[1] * w_out[1])
    lane = lax.broadcasted_iota(jnp.int32, (1, 128), 1)
    row = jnp.zeros((1, 128), F32)
    for at, value in enumerate((gamma_ref[...], curve_ref[...], inner_ref[:8], inner_ref[8:], cross, own)):
        row = jnp.where(lane == at, jnp.sum(value), row)
    sums[...] = jnp.broadcast_to(row[None], sums.shape)


def spread_slices(coefs, parts, cut):
    totals = [None] * 12
    for r in range(ANG):
        for i in range(PAIR):
            value = parts[r][i, :, cut].astype(F32)
            for e in range(12):
                term = coefs[r, i, e:e + 1, :] * value
                totals[e] = term if totals[e] is None else totals[e] + term
    return totals


def is_even(flag, columns=CH):
    return jnp.concatenate([flag[...]] * (columns // 128), axis=1) == 0


def cuts():
    return [pl.ds(at * CH, CH) for at in range(Q // CH)]


def combine_parts(flag, coefs, parts, mine, sent):
    even = is_even(flag)
    for cut in cuts():
        totals = spread_slices(coefs, parts, cut)
        for e, total in enumerate(totals):
            mine[e, :, cut] = total
        for z in range(ZD):
            sent[z, :, cut] = totals[4 + z].astype(BF16)
            sent[ZD + z, :, cut] = jnp.where(even, totals[8 + z], totals[z]).astype(BF16)


def open_kernel(flag, c0, c1, c2, c3, mine, sent, coefs):
    parts = (c0, c1, c2, c3)
    for r in range(ANG):
        for i in range(PAIR):
            value = parts[r][i, :, Q:Q + 128].astype(F32)
            value = value + parts[r][i, :, Q + 128:Q + 256].astype(F32)
            coefs[r, i] = value + parts[r][i, :, Q + 256:].astype(F32)
    combine_parts(flag, coefs, parts, mine, sent)


def combine_kernel(flag, coefs, c0, c1, c2, c3, mine, sent):
    combine_parts(flag, coefs, (c0, c1, c2, c3), mine, sent)


def edge_kernel(flag, mine, other, sent):
    even = is_even(flag, Q)
    for z in range(ZD):
        sent[z] = (mine[4 + z] + other[ZD + z].astype(F32)).astype(BF16)
        sent[ZD + z] = jnp.where(even, mine[z], mine[8 + z]).astype(BF16)


def pieces_body(flag, coefs, mine, other, outer, inner, g_out, outs, kept, note):
    even = is_even(flag)
    for cut in cuts():
        def get(ref, z):
            return ref[z, :, cut].astype(F32)

        cells = [None] * 12
        for z in range(ZD):
            beyond = get(outer, z)
            beside = get(other, z) + get(inner, 4 + z)
            cells[z] = mine[z, :, cut] + jnp.where(even, beyond, beside)
            cells[4 + z] = mine[4 + z, :, cut] + get(other, 4 + z) + get(outer, 4 + z)
            cells[8 + z] = mine[8 + z, :, cut] + jnp.where(even, beside, beyond)
            g_out[z, :, cut] = cells[4 + z]
            kept = note(kept, z, cut, cells[4 + z])
        for r in range(ANG):
            for i in range(PAIR):
                total = None
                for e in range(12):
                    term = coefs[r, i, e:e + 1, :] * cells[e]
                    total = term if total is None else total + term
                outs[r][i, :, cut] = total.astype(outs[r].dtype)
    return kept


def pieces_first(flag, coefs, mine, other, outer, inner, g_out, h0, h1, h2, h3, dots):
    def note(kept, z, cut, value):
        return kept + fold(value * value)

    dots[...] = pieces_body(
        flag, coefs, mine, other, outer, inner, g_out, (h0, h1, h2, h3), jnp.zeros((8, 128), F32), note
    )


def pieces_second(flag, coefs, g0, mine, other, outer, inner, g_out, h0, h1, h2, h3, dots):
    def note(kept, z, cut, value):
        return kept[0] + fold(value * g0[z, :, cut]), kept[1] + fold(value * value)

    dots[:8], dots[8:] = pieces_body(
        flag, coefs, mine, other, outer, inner, g_out, (h0, h1, h2, h3), (jnp.zeros((8, 128), F32),) * 2, note
    )


def last_kernel(flag, coefs, c0, c1, c2, c3, own, inner, outer):
    even = is_even(flag)
    for cut in cuts():
        totals = spread_slices(coefs, (c0, c1, c2, c3), cut)
        for z in range(ZD):
            own[z, :, cut] = totals[4 + z]
            inner[z, :, cut] = jnp.where(even, totals[8 + z], totals[z])
            outer[z, :, cut] = jnp.where(even, totals[z], totals[8 + z])


def steps(sums_ref):
    total = sums_ref[0]
    for at in range(1, sums_ref.shape[0]):
        total = total + sums_ref[at]
    lane = lax.broadcasted_iota(jnp.int32, (1, 128), 1)
    gamma0, curve0, inner, norm, cross, own = [
        jnp.sum(jnp.where(lane == at, total, 0.0)) for at in range(6)
    ]
    step0 = gamma0 / curve0
    gamma1 = gamma0 - 2.0 * step0 * inner + step0 * step0 * norm
    ratio = gamma1 / gamma0
    curve1 = (1.0 + ratio) * (1.0 + ratio) * curve0 - 2.0 * (1.0 + ratio) * step0 * cross + step0 * step0 * own
    step1 = gamma1 / curve1
    return step0 + step1 * (1.0 + ratio), step0 * step1


def volume_kernel(sums, g0, z0, out):
    one, two = steps(sums)
    for z in range(ZD):
        out[z] = (one * g0[z] - two * z0[z]).astype(BF16)


def gradient_kernel(sums, t1, inner, outer, g0, z0, out):
    one, two = steps(sums)
    for z in range(ZD):
        last = t1[z] + inner[z] + outer[z]
        out[z] = (g0[z] - one * z0[z] + two * last).astype(BF16)


def residual_kernel(sums, p, q0, w0, out):
    one, two = steps(sums)
    for a in range(PAIR):
        out[a, 0] = p[a, 0] - one * q0[a] + two * w0[a]


def place_kernel(me_ref, s0, s1, s2, s3, out):
    def place(at, share):
        out[:, :, at] = share[...].astype(F32)

    gather_shares(me_ref[0], (s0, s1, s2, s3), place)


def along_ang(value, other):
    return lax.ppermute(value, "ang", [(i, i ^ other) for i in range(ANG)])


def on_chip(value):
    return lax.ppermute(value, "slab", [(i, i ^ 1) for i in range(lax.axis_size("slab"))])


def across(value):
    count = lax.axis_size("slab")
    return lax.ppermute(
        value, "slab", [pair for i in range(1, count - 1, 2) for pair in ((i, i + 1), (i + 1, i))]
    )


def exchange(shares):
    return (shares[0],) + tuple(along_ang(shares[i], ORDER[i]) for i in range(1, ANG))


def per_device(projections, weights, columns, row_weights, reach):
    me = lax.axis_index("ang").astype(jnp.int32).reshape(1)
    parity = (lax.axis_index("slab").astype(jnp.int32) & 1).reshape(1)
    row = sds((PAIR * ZD, 128), F32)
    inner, own, outer, flag, cols, p = call(
        open_inputs, [row] * 3 + [sds((L, 128), jnp.int32), sds((3, PAIR, UB), jnp.int32), sds(projections.shape, F32)], [SMEM] + [HBM] * 4,
        [pltpu.SMEM(row_weights.shape, F32), pltpu.SMEM(reach.shape, jnp.int32), pltpu.SemaphoreType.DMA((4,))],
        limit=53,
    )(parity, row_weights, reach, columns.transpose(2, 0, 1), projections)
    outer = across(outer)
    edges = (flag, own, on_chip(inner), outer)

    def share(dtype, more=0):
        return sds((PAIR, L, Q + more), dtype)

    full = sds((PAIR, L, X), F32)
    part = sds((ZD, L, Q), F32)
    part_b = sds((ZD, L, Q), BF16)
    acc = pltpu.VMEM((PAIR, L, X), F32)
    macs = 2 * PAIR * L * UB * 384 * 128
    sent = [sds((3 * ZD, L, Q), F32), sds((2 * ZD, L, Q), BF16)]

    def halo(mine, sent):
        other = on_chip(sent)
        (edge,) = call(edge_kernel, [sds((2 * ZD, L, Q), BF16)], [VMEM] * 3)(flag, mine, other)
        outer = across(edge)
        return mine, other, outer, on_chip(outer)

    *shares, w = call(
        back_kernel, [share(BF16)] * 4 + [sds((PAIR, UB, 384, 128), BF16)],
        [SMEM] * 2 + [VMEM, HBM], [acc, pltpu.SemaphoreType.DMA((PAIR, UB // CHUNK))],
        flops=2 * macs, nbytes=7_000_000, limit=46,
    )(me, cols, p, weights.reshape(PAIR, UB, 384, 128))
    shares = call(stencil_kernel, [share(BF16, COEF)] * 4, [VMEM] * 8)(*edges, *shares)
    *spread, coefs = call(
        open_kernel, sent + [sds((ANG, PAIR, L, 128), F32)], [VMEM] * 5, flops=10_000_000
    )(flag, *exchange(shares))
    g0, *shares, gamma = call(
        pieces_first, [part] + [share(BF16)] * 4 + [sds((8, 128), F32)], [VMEM] * 6, flops=10_000_000
    )(flag, coefs, *halo(*spread))

    *shares, q0, curve = call(
        first_kernel, [share(MID)] * 4 + [full, sds((8, 128), F32)],
        [SMEM] * 2 + [VMEM] * 5, [pltpu.VMEM((PAIR, L, X), BF16), acc],
        flops=3 * macs, nbytes=7_000_000,
    )(me, cols, *exchange(shares), w)
    spread = call(combine_kernel, sent, [VMEM] * 6, flops=10_000_000)(flag, coefs, *exchange(shares))
    z0, *shares, inner = call(
        pieces_second, [part] + [share(BF16)] * 4 + [sds((16, 128), F32)], [VMEM] * 7, flops=10_000_000
    )(flag, coefs, g0, *halo(*spread))

    *shares, w0, sums = call(
        second_kernel, [share(F32)] * 4 + [full, sds((lax.axis_size("slab") * ANG, 1, 128), F32)],
        [SMEM] * 2 + [VMEM] * 9, [pltpu.VMEM((PAIR, L, X), BF16), acc],
        flops=4 * macs, nbytes=9_000_000,
    )(me, cols, *exchange(shares), q0, gamma, curve, inner, w)
    shares = exchange(shares)
    sums = lax.all_to_all(sums, ("slab", "ang"), 0, 0, tiled=True)
    own, inner, outer = call(last_kernel, [part] * 3, [VMEM] * 6, flops=10_000_000)(flag, coefs, *shares)
    outer = across(outer)
    inner = on_chip(inner)
    (volume,) = call(volume_kernel, [part_b], [VMEM] * 3)(sums, g0, z0)
    (residual,) = call(residual_kernel, [sds(projections.shape, F32)], [VMEM] * 4)(sums, projections, q0, w0)
    volume = exchange((volume,) * 4)
    (gradient,) = call(gradient_kernel, [part_b], [VMEM] * 6)(sums, own, inner, outer, g0, z0)
    whole = [sds((ZD, L, X), F32)]
    (volume,) = call(place_kernel, whole, [SMEM] + [VMEM] * 4)(me, *volume)
    (gradient,) = call(place_kernel, whole, [SMEM] + [VMEM] * 4)(me, *exchange((gradient,) * 4))
    return volume, residual, gradient


def solution(mesh):
    in_specs = (
        P("ang", "slab", None, None),
        P("ang", None, None, None, None),
        P("ang", None, None),
        P("ang", "slab", None, None, None),
        P("ang", "slab", None),
    )
    out_specs = (P("slab", None, None), P("ang", "slab", None, None), P("slab", None, None))
    return jax.shard_map(
        per_device, mesh=mesh, in_specs=in_specs, out_specs=out_specs, check_vma=False
    )
```

```python
import functools

import jax
import jax.numpy as jnp
from jax import lax
from jax.experimental import pallas as pl
from jax.experimental.pallas import tpu as pltpu
from jax.sharding import PartitionSpec as P

F32 = jnp.float32
BF16 = jnp.bfloat16
ANG = 4
ORDER = (0, 2, 3, 1)
PAIR = 2
L = 16
X = 4096
Q = X // ANG
UB = 32
ZD = 4
CH = 128
COEF = 128
CHUNK = 16
GROUP = 8
VMEM = pl.BlockSpec(memory_space=pltpu.VMEM)
SMEM = pl.BlockSpec(memory_space=pltpu.SMEM)
MID = BF16
HBM = pl.BlockSpec(memory_space=pltpu.HBM)


def call(kernel, outs, specs, scratch=(), flops=0, nbytes=2_000_000, limit=24):
    return pl.pallas_call(
        kernel,
        out_shape=outs,
        in_specs=specs,
        out_specs=[VMEM] * len(outs),
        scratch_shapes=list(scratch),
        compiler_params=pltpu.CompilerParams(vmem_limit_bytes=limit * 1024 * 1024),
        cost_estimate=pl.CostEstimate(flops=flops, bytes_accessed=nbytes, transcendentals=0),
    )


def sds(shape, dtype):
    return jax.ShapeDtypeStruct(shape, dtype)


def halves(value):
    high = value.astype(BF16)
    low = (value - high.astype(F32)).astype(BF16)
    return jnp.concatenate([high, low], axis=0)


def fold(value):
    total = value[:8] + value[8:]
    out = total[:, :128]
    for at in range(1, total.shape[1] // 128):
        out = out + total[:, 128 * at:128 * (at + 1)]
    return out


def window(cols, a, block):
    return pl.ds(pl.multiple_of(cols[0, a, block] * 128, 128), 384)


def back_block(a, block, value, cols, w, acc):
    both = halves(value)
    spread = lax.dot_general(
        both, w[a, block], (((1,), (1,)), ((), ())), preferred_element_type=F32
    )
    at = window(cols, a, block)
    acc[a, :, at] += spread[:L] + spread[L:]


def send_shares(me, acc, outs):
    for r in range(ANG):
        quarter = me ^ ORDER[r]
        share = acc[:, :, pl.ds(pl.multiple_of(quarter * Q, Q), Q)]
        outs[r][:, :, :Q] = share.astype(outs[r].dtype)


def open_inputs(parity, rows_hbm, reach_hbm, cols_hbm, p_hbm, inner, own, outer, flag, cols, p, rows, reach, sem):
    copies = [
        pltpu.make_async_copy(src, dst, sem.at[at])
        for at, (src, dst) in enumerate(((rows_hbm, rows), (reach_hbm, reach), (cols_hbm, cols), (p_hbm, p)))
    ]
    for copy in copies:
        copy.start()
    copies[0].wait()
    copies[1].wait()
    flag[...] = jnp.full((L, 128), parity[0], jnp.int32)
    even = parity[0] == 0
    for i in range(PAIR):
        for z in range(ZD):
            top = jnp.where(reach[i, 0, 1] == 1, rows[i, 0, 2, 0, z], 0.0)
            low = jnp.where(reach[i, 0, 0] == -1, rows[i, 0, 0, 0, z], 0.0)
            at = slice(ZD * i + z, ZD * i + z + 1)
            inner[at] = jnp.full((1, 128), jnp.where(even, top, low), F32)
            outer[at] = jnp.full((1, 128), jnp.where(even, low, top), F32)
            own[at] = jnp.full((1, 128), rows[i, 0, 1, 0, z], F32)
    copies[2].wait()
    copies[3].wait()


def back_kernel(me_ref, cols, p_ref, w_hbm, o0, o1, o2, o3, w, acc, sem):
    copies = []
    for a in range(PAIR):
        for g in range(UB // CHUNK):
            span = pl.ds(CHUNK * g, CHUNK)
            copies.append(pltpu.make_async_copy(w_hbm.at[a, span], w.at[a, span], sem.at[a, g]))
            copies[-1].start()
    acc[...] = jnp.zeros_like(acc)
    for a in range(PAIR):
        for block in range(UB):
            if block % CHUNK == 0:
                copies[(a * UB + block) // CHUNK].wait()
            back_block(a, block, p_ref[a, 0, :, 128 * block:128 * (block + 1)], cols, w, acc)
    send_shares(me_ref[0], acc, (o0, o1, o2, o3))


def stencil_kernel(flag, own, inner, outer, c0, c1, c2, c3, o0, o1, o2, o3):
    outs = (o0, o1, o2, o3)
    for share, out in zip((c0, c1, c2, c3), outs):
        out[:, :, :Q] = share[...]
    even = flag[:8] == 0
    from_low = jnp.where(even, outer[...], inner[...])
    from_high = jnp.where(even, inner[...], outer[...])
    for i in range(PAIR):
        at = slice(ZD * i, ZD * (i + 1))
        rest = jnp.concatenate([from_low[at], own[at], from_high[at], jnp.zeros((4, 128), F32)], axis=0)
        lane = lax.broadcasted_iota(jnp.int32, (L, 128), 1)
        packed = jnp.zeros((L, 128), F32)
        for part in range(3):
            piece = rest.astype(BF16).astype(F32)
            rest = rest - piece
            packed = jnp.where(lane == part, piece, packed)
        for out in outs:
            out[i, :, Q:] = packed.astype(BF16)


def both_body(cols, w, acc, lhs, store):
    acc[...] = jnp.zeros_like(acc)
    for a in range(PAIR):
        for g in range(UB // GROUP):
            images = []
            for i in range(GROUP):
                block = g * GROUP + i
                image = jnp.dot(lhs(a, window(cols, a, block)), w[a, block], preferred_element_type=F32)
                if image.shape[0] > L:
                    image = image[:L] + image[L:]
                store(a, block, image)
                images.append(image)
            for i in range(GROUP):
                back_block(a, g * GROUP + i, images[i], cols, w, acc)


def gather_shares(me, shares, place):
    for r in range(ANG):
        quarter = me ^ ORDER[r]
        place(pl.ds(pl.multiple_of(quarter * Q, Q), Q), shares[r])


def first_kernel(me_ref, cols, h0, h1, h2, h3, w, o0, o1, o2, o3, q_out, dots, hb, acc):

    def place(at, share):
        hb[:, :, at] = share[...]

    def store(a, block, image):
        q_out[a, :, 128 * block:128 * (block + 1)] = image

    gather_shares(me_ref[0], (h0, h1, h2, h3), place)
    both_body(cols, w, acc, lambda a, at: hb[a, :, at], store)
    send_shares(me_ref[0], acc, (o0, o1, o2, o3))
    dots[...] = fold(q_out[0] * q_out[0]) + fold(q_out[1] * q_out[1])


def second_kernel(me_ref, cols, h0, h1, h2, h3, q0_ref, gamma_ref, curve_ref, inner_ref, w,
                  o0, o1, o2, o3, w_out, sums, hb, acc):

    def place(at, share):
        hb[:, :, at] = share[...]

    def store(a, block, image):
        w_out[a, :, 128 * block:128 * (block + 1)] = image

    gather_shares(me_ref[0], (h0, h1, h2, h3), place)
    both_body(cols, w, acc, lambda a, at: hb[a, :, at], store)
    send_shares(me_ref[0], acc, (o0, o1, o2, o3))
    cross = fold(w_out[0] * q0_ref[0]) + fold(w_out[1] * q0_ref[1])
    own = fold(w_out[0] * w_out[0]) + fold(w_out[1] * w_out[1])
    lane = lax.broadcasted_iota(jnp.int32, (1, 128), 1)
    row = jnp.zeros((1, 128), F32)
    for at, value in enumerate((gamma_ref[...], curve_ref[...], inner_ref[:8], inner_ref[8:], cross, own)):
        row = jnp.where(lane == at, jnp.sum(value), row)
    sums[...] = jnp.broadcast_to(row[None], sums.shape)


def spread_slices(coefs, parts, cut):
    totals = [None] * 12
    for r in range(ANG):
        for i in range(PAIR):
            value = parts[r][i, :, cut].astype(F32)
            for e in range(12):
                term = coefs[r, i, e:e + 1, :] * value
                totals[e] = term if totals[e] is None else totals[e] + term
    return totals


def is_even(flag, columns=CH):
    return jnp.concatenate([flag[...]] * (columns // 128), axis=1) == 0


def cuts():
    return [pl.ds(at * CH, CH) for at in range(Q // CH)]


def combine_parts(flag, coefs, parts, mine, sent):
    even = is_even(flag)
    for cut in cuts():
        totals = spread_slices(coefs, parts, cut)
        for e, total in enumerate(totals):
            mine[e, :, cut] = total
        for z in range(ZD):
            sent[z, :, cut] = totals[4 + z].astype(BF16)
            sent[ZD + z, :, cut] = jnp.where(even, totals[8 + z], totals[z]).astype(BF16)


def open_kernel(flag, c0, c1, c2, c3, mine, sent, coefs):
    parts = (c0, c1, c2, c3)
    for r in range(ANG):
        for i in range(PAIR):
            value = parts[r][i, :, Q:].astype(F32)
            total = value[:, 0:1] + value[:, 1:2] + value[:, 2:3]
            coefs[r, i] = jnp.broadcast_to(total, (L, 128))
    combine_parts(flag, coefs, parts, mine, sent)


def combine_kernel(flag, coefs, c0, c1, c2, c3, mine, sent):
    combine_parts(flag, coefs, (c0, c1, c2, c3), mine, sent)


def edge_kernel(flag, mine, other, sent):
    even = is_even(flag, Q)
    for z in range(ZD):
        sent[z] = (mine[4 + z] + other[ZD + z].astype(F32)).astype(BF16)
        sent[ZD + z] = jnp.where(even, mine[z], mine[8 + z]).astype(BF16)


def pieces_body(flag, coefs, mine, other, outer, inner, g_out, outs, kept, note):
    even = is_even(flag)
    for cut in cuts():
        def get(ref, z):
            return ref[z, :, cut].astype(F32)

        cells = [None] * 12
        for z in range(ZD):
            beyond = get(outer, z)
            beside = get(other, z) + get(inner, 4 + z)
            cells[z] = mine[z, :, cut] + jnp.where(even, beyond, beside)
            cells[4 + z] = mine[4 + z, :, cut] + get(other, 4 + z) + get(outer, 4 + z)
            cells[8 + z] = mine[8 + z, :, cut] + jnp.where(even, beside, beyond)
            g_out[z, :, cut] = cells[4 + z]
            kept = note(kept, z, cut, cells[4 + z])
        for r in range(ANG):
            for i in range(PAIR):
                total = None
                for e in range(12):
                    term = coefs[r, i, e:e + 1, :] * cells[e]
                    total = term if total is None else total + term
                outs[r][i, :, cut] = total.astype(outs[r].dtype)
    return kept


def pieces_first(flag, coefs, mine, other, outer, inner, g_out, h0, h1, h2, h3, dots):
    def note(kept, z, cut, value):
        return kept + fold(value * value)

    dots[...] = pieces_body(
        flag, coefs, mine, other, outer, inner, g_out, (h0, h1, h2, h3), jnp.zeros((8, 128), F32), note
    )


def pieces_second(flag, coefs, g0, mine, other, outer, inner, g_out, h0, h1, h2, h3, dots):
    def note(kept, z, cut, value):
        return kept[0] + fold(value * g0[z, :, cut]), kept[1] + fold(value * value)

    dots[:8], dots[8:] = pieces_body(
        flag, coefs, mine, other, outer, inner, g_out, (h0, h1, h2, h3), (jnp.zeros((8, 128), F32),) * 2, note
    )


def last_kernel(flag, coefs, c0, c1, c2, c3, own, inner, outer):
    even = is_even(flag)
    for cut in cuts():
        totals = spread_slices(coefs, (c0, c1, c2, c3), cut)
        for z in range(ZD):
            own[z, :, cut] = totals[4 + z]
            inner[z, :, cut] = jnp.where(even, totals[8 + z], totals[z])
            outer[z, :, cut] = jnp.where(even, totals[z], totals[8 + z])


def steps(sums_ref):
    parts = [sums_ref[at] for at in range(16)]
    for at in range(16, sums_ref.shape[0]):
        parts[at % 16] = parts[at % 16] + sums_ref[at]
    while len(parts) > 1:
        parts = [low + high for low, high in zip(parts[::2], parts[1::2])]
    total = parts[0]
    lane = lax.broadcasted_iota(jnp.int32, (1, 128), 1)
    gamma0, curve0, inner, norm, cross, own = [
        jnp.sum(jnp.where(lane == at, total, 0.0)) for at in range(6)
    ]
    step0 = gamma0 / curve0
    gamma1 = gamma0 - 2.0 * step0 * inner + step0 * step0 * norm
    ratio = gamma1 / gamma0
    curve1 = (1.0 + ratio) * (1.0 + ratio) * curve0 - 2.0 * (1.0 + ratio) * step0 * cross + step0 * step0 * own
    step1 = gamma1 / curve1
    return step0 + step1 * (1.0 + ratio), step0 * step1


def volume_kernel(sums, g0, z0, out):
    one, two = steps(sums)
    for z in range(ZD):
        out[z] = (one * g0[z] - two * z0[z]).astype(BF16)


def gradient_kernel(sums, t1, inner, outer, g0, z0, out):
    one, two = steps(sums)
    for z in range(ZD):
        last = t1[z] + inner[z] + outer[z]
        out[z] = (g0[z] - one * z0[z] + two * last).astype(BF16)


def residual_kernel(sums, p, q0, w0, out):
    one, two = steps(sums)
    for a in range(PAIR):
        out[a, 0] = p[a, 0] - one * q0[a] + two * w0[a]


def place_kernel(me_ref, s0, s1, s2, s3, out):
    def place(at, share):
        out[:, :, at] = share[...].astype(F32)

    gather_shares(me_ref[0], (s0, s1, s2, s3), place)


def along_ang(value, other):
    return lax.ppermute(value, "ang", [(i, i ^ other) for i in range(ANG)])


def on_chip(value):
    return lax.ppermute(value, "slab", [(i, i ^ 1) for i in range(lax.axis_size("slab"))])


def across(value):
    count = lax.axis_size("slab")
    return lax.ppermute(
        value, "slab", [pair for i in range(1, count - 1, 2) for pair in ((i, i + 1), (i + 1, i))]
    )


def exchange(shares):
    return (shares[0],) + tuple(along_ang(shares[i], ORDER[i]) for i in range(1, ANG))


def per_device(projections, weights, columns, row_weights, reach):
    me = lax.axis_index("ang").astype(jnp.int32).reshape(1)
    parity = (lax.axis_index("slab").astype(jnp.int32) & 1).reshape(1)
    row = sds((PAIR * ZD, 128), F32)
    inner, own, outer, flag, cols, p = call(
        open_inputs, [row] * 3 + [sds((L, 128), jnp.int32), sds((3, PAIR, UB), jnp.int32), sds(projections.shape, F32)], [SMEM] + [HBM] * 4,
        [pltpu.SMEM(row_weights.shape, F32), pltpu.SMEM(reach.shape, jnp.int32), pltpu.SemaphoreType.DMA((4,))],
        limit=53,
    )(parity, row_weights, reach, columns.transpose(2, 0, 1), projections)
    outer = across(outer)
    edges = (flag, own, on_chip(inner), outer)

    def share(dtype, more=0):
        return sds((PAIR, L, Q + more), dtype)

    full = sds((PAIR, L, X), F32)
    part = sds((ZD, L, Q), F32)
    part_b = sds((ZD, L, Q), BF16)
    acc = pltpu.VMEM((PAIR, L, X), F32)
    macs = 2 * PAIR * L * UB * 384 * 128
    sent = [sds((3 * ZD, L, Q), F32), sds((2 * ZD, L, Q), BF16)]

    def halo(mine, sent):
        other = on_chip(sent)
        (edge,) = call(edge_kernel, [sds((2 * ZD, L, Q), BF16)], [VMEM] * 3)(flag, mine, other)
        outer = across(edge)
        return mine, other, outer, on_chip(outer)

    *shares, w = call(
        back_kernel, [share(BF16)] * 4 + [sds((PAIR, UB, 384, 128), BF16)],
        [SMEM] * 2 + [VMEM, HBM], [acc, pltpu.SemaphoreType.DMA((PAIR, UB // CHUNK))],
        flops=2 * macs, nbytes=7_000_000, limit=46,
    )(me, cols, p, weights.reshape(PAIR, UB, 384, 128))
    shares = call(stencil_kernel, [share(BF16, COEF)] * 4, [VMEM] * 8)(*edges, *shares)
    *spread, coefs = call(
        open_kernel, sent + [sds((ANG, PAIR, L, 128), F32)], [VMEM] * 5, flops=10_000_000
    )(flag, *exchange(shares))
    g0, *shares, gamma = call(
        pieces_first, [part] + [share(BF16)] * 4 + [sds((8, 128), F32)], [VMEM] * 6, flops=10_000_000
    )(flag, coefs, *halo(*spread))

    *shares, q0, curve = call(
        first_kernel, [share(MID)] * 4 + [full, sds((8, 128), F32)],
        [SMEM] * 2 + [VMEM] * 5, [pltpu.VMEM((PAIR, L, X), BF16), acc],
        flops=3 * macs, nbytes=7_000_000,
    )(me, cols, *exchange(shares), w)
    spread = call(combine_kernel, sent, [VMEM] * 6, flops=10_000_000)(flag, coefs, *exchange(shares))
    z0, *shares, inner = call(
        pieces_second, [part] + [share(BF16)] * 4 + [sds((16, 128), F32)], [VMEM] * 7, flops=10_000_000
    )(flag, coefs, g0, *halo(*spread))

    *shares, w0, sums = call(
        second_kernel, [share(F32)] * 4 + [full, sds((lax.axis_size("slab") * ANG, 1, 128), F32)],
        [SMEM] * 2 + [VMEM] * 9, [pltpu.VMEM((PAIR, L, X), BF16), acc],
        flops=4 * macs, nbytes=9_000_000,
    )(me, cols, *exchange(shares), q0, gamma, curve, inner, w)
    shares = exchange(shares)
    sums = lax.all_to_all(sums, ("slab", "ang"), 0, 0, tiled=True)
    own, inner, outer = call(last_kernel, [part] * 3, [VMEM] * 6, flops=10_000_000)(flag, coefs, *shares)
    outer = across(outer)
    inner = on_chip(inner)
    (volume,) = call(volume_kernel, [part_b], [VMEM] * 3)(sums, g0, z0)
    (residual,) = call(residual_kernel, [sds(projections.shape, F32)], [VMEM] * 4)(sums, projections, q0, w0)
    volume = exchange((volume,) * 4)
    (gradient,) = call(gradient_kernel, [part_b], [VMEM] * 6)(sums, own, inner, outer, g0, z0)
    whole = [sds((ZD, L, X), F32)]
    (volume,) = call(place_kernel, whole, [SMEM] + [VMEM] * 4)(me, *volume)
    (gradient,) = call(place_kernel, whole, [SMEM] + [VMEM] * 4)(me, *exchange((gradient,) * 4))
    return volume, residual, gradient


def solution(mesh):
    in_specs = (
        P("ang", "slab", None, None),
        P("ang", None, None, None, None),
        P("ang", None, None),
        P("ang", "slab", None, None, None),
        P("ang", "slab", None),
    )
    out_specs = (P("slab", None, None), P("ang", "slab", None, None), P("slab", None, None))
    return jax.shard_map(
        per_device, mesh=mesh, in_specs=in_specs, out_specs=out_specs, check_vma=False
    )
```

```python
import functools

import jax
import jax.numpy as jnp
from jax import lax
from jax.experimental import pallas as pl
from jax.experimental.pallas import tpu as pltpu
from jax.sharding import PartitionSpec as P

F32 = jnp.float32
BF16 = jnp.bfloat16
ANG = 4
ORDER = (0, 2, 3, 1)
PAIR = 2
L = 16
X = 4096
Q = X // ANG
UB = 32
ZD = 4
CH = 128
COEF = 128
CHUNK = 16
GROUP = 8
VMEM = pl.BlockSpec(memory_space=pltpu.VMEM)
SMEM = pl.BlockSpec(memory_space=pltpu.SMEM)
MID = BF16
HBM = pl.BlockSpec(memory_space=pltpu.HBM)


def call(kernel, outs, specs, scratch=(), flops=0, nbytes=2_000_000, limit=24):
    return pl.pallas_call(
        kernel,
        out_shape=outs,
        in_specs=specs,
        out_specs=[VMEM] * len(outs),
        scratch_shapes=list(scratch),
        compiler_params=pltpu.CompilerParams(vmem_limit_bytes=limit * 1024 * 1024),
        cost_estimate=pl.CostEstimate(flops=flops, bytes_accessed=nbytes, transcendentals=0),
    )


def sds(shape, dtype):
    return jax.ShapeDtypeStruct(shape, dtype)


def halves(value):
    high = value.astype(BF16)
    low = (value - high.astype(F32)).astype(BF16)
    return jnp.concatenate([high, low], axis=0)


def fold(value):
    total = value[:8] + value[8:]
    out = total[:, :128]
    for at in range(1, total.shape[1] // 128):
        out = out + total[:, 128 * at:128 * (at + 1)]
    return out


def window(cols, a, block):
    return pl.ds(pl.multiple_of(cols[0, a, block] * 128, 128), 384)


def back_block(a, block, value, cols, w, acc):
    both = halves(value)
    spread = lax.dot_general(
        both, w[a, block], (((1,), (1,)), ((), ())), preferred_element_type=F32
    )
    at = window(cols, a, block)
    acc[a, :, at] += spread[:L] + spread[L:]


def send_shares(me, acc, outs):
    for r in range(ANG):
        quarter = me ^ ORDER[r]
        share = acc[:, :, pl.ds(pl.multiple_of(quarter * Q, Q), Q)]
        outs[r][:, :, :Q] = share.astype(outs[r].dtype)


def open_inputs(parity, rows_hbm, reach_hbm, cols_hbm, p_hbm, inner, own, outer, flag, cols, p, rows, reach, sem):
    copies = [
        pltpu.make_async_copy(src, dst, sem.at[at])
        for at, (src, dst) in enumerate(((rows_hbm, rows), (reach_hbm, reach), (cols_hbm, cols), (p_hbm, p)))
    ]
    for copy in copies:
        copy.start()
    copies[0].wait()
    copies[1].wait()
    flag[...] = jnp.full((L, 128), parity[0], jnp.int32)
    even = parity[0] == 0
    for i in range(PAIR):
        for z in range(ZD):
            top = jnp.where(reach[i, 0, 1] == 1, rows[i, 0, 2, 0, z], 0.0)
            low = jnp.where(reach[i, 0, 0] == -1, rows[i, 0, 0, 0, z], 0.0)
            at = slice(ZD * i + z, ZD * i + z + 1)
            inner[at] = jnp.full((1, 128), jnp.where(even, top, low), F32)
            outer[at] = jnp.full((1, 128), jnp.where(even, low, top), F32)
            own[at] = jnp.full((1, 128), rows[i, 0, 1, 0, z], F32)
    copies[2].wait()
    copies[3].wait()


def back_kernel(me_ref, cols, p_ref, w_hbm, o0, o1, o2, o3, w, acc, sem):
    copies = []
    for a in range(PAIR):
        for g in range(UB // CHUNK):
            span = pl.ds(CHUNK * g, CHUNK)
            copies.append(pltpu.make_async_copy(w_hbm.at[a, span], w.at[a, span], sem.at[a, g]))
            copies[-1].start()
    acc[...] = jnp.zeros_like(acc)
    for a in range(PAIR):
        for block in range(UB):
            if block % CHUNK == 0:
                copies[(a * UB + block) // CHUNK].wait()
            back_block(a, block, p_ref[a, 0, :, 128 * block:128 * (block + 1)], cols, w, acc)
    send_shares(me_ref[0], acc, (o0, o1, o2, o3))


def stencil_kernel(flag, own, inner, outer, c0, c1, c2, c3, o0, o1, o2, o3):
    outs = (o0, o1, o2, o3)
    for share, out in zip((c0, c1, c2, c3), outs):
        out[:, :, :Q] = share[...]
    even = flag[:8] == 0
    from_low = jnp.where(even, outer[...], inner[...])
    from_high = jnp.where(even, inner[...], outer[...])
    for i in range(PAIR):
        at = slice(ZD * i, ZD * (i + 1))
        rest = jnp.concatenate([from_low[at], own[at], from_high[at], jnp.zeros((4, 128), F32)], axis=0)
        lane = lax.broadcasted_iota(jnp.int32, (L, 128), 1)
        packed = jnp.zeros((L, 128), F32)
        for part in range(3):
            piece = rest.astype(BF16).astype(F32)
            rest = rest - piece
            packed = jnp.where(lane == part, piece, packed)
        for out in outs:
            out[i, :, Q:] = packed.astype(BF16)


def both_body(cols, w, acc, lhs, store):
    acc[...] = jnp.zeros_like(acc)
    for a in range(PAIR):
        for g in range(UB // GROUP):
            images = []
            for i in range(GROUP):
                block = g * GROUP + i
                image = jnp.dot(lhs(a, window(cols, a, block)), w[a, block], preferred_element_type=F32)
                if image.shape[0] > L:
                    image = image[:L] + image[L:]
                store(a, block, image)
                images.append(image)
            for i in range(GROUP):
                back_block(a, g * GROUP + i, images[i], cols, w, acc)


def gather_shares(me, shares, place):
    for r in range(ANG):
        quarter = me ^ ORDER[r]
        place(pl.ds(pl.multiple_of(quarter * Q, Q), Q), shares[r])


def first_kernel(me_ref, cols, h0, h1, h2, h3, w, o0, o1, o2, o3, q_out, dots, hb, acc):

    def place(at, share):
        hb[:, :, at] = share[...]

    def store(a, block, image):
        q_out[a, :, 128 * block:128 * (block + 1)] = image

    gather_shares(me_ref[0], (h0, h1, h2, h3), place)
    both_body(cols, w, acc, lambda a, at: hb[a, :, at], store)
    send_shares(me_ref[0], acc, (o0, o1, o2, o3))
    dots[...] = fold(q_out[0] * q_out[0]) + fold(q_out[1] * q_out[1])


def second_kernel(me_ref, cols, h0, h1, h2, h3, q0_ref, gamma_ref, curve_ref, inner_ref, w,
                  o0, o1, o2, o3, w_out, sums, hb, acc):

    def place(at, share):
        hb[:, :, at] = share[...]

    def store(a, block, image):
        w_out[a, :, 128 * block:128 * (block + 1)] = image

    gather_shares(me_ref[0], (h0, h1, h2, h3), place)
    both_body(cols, w, acc, lambda a, at: hb[a, :, at], store)
    send_shares(me_ref[0], acc, (o0, o1, o2, o3))
    cross = fold(w_out[0] * q0_ref[0]) + fold(w_out[1] * q0_ref[1])
    own = fold(w_out[0] * w_out[0]) + fold(w_out[1] * w_out[1])
    lane = lax.broadcasted_iota(jnp.int32, (1, 128), 1)
    row = jnp.zeros((1, 128), F32)
    for at, value in enumerate((gamma_ref[...], curve_ref[...], inner_ref[:8], inner_ref[8:], cross, own)):
        row = jnp.where(lane == at, jnp.sum(value), row)
    sums[...] = jnp.broadcast_to(row[None], sums.shape)


def spread_slices(coefs, parts, cut):
    totals = [None] * 12
    for r in range(ANG):
        for i in range(PAIR):
            value = parts[r][i, :, cut].astype(F32)
            for e in range(12):
                term = coefs[r, i, e:e + 1, :] * value
                totals[e] = term if totals[e] is None else totals[e] + term
    return totals


def is_even(flag, columns=CH):
    return jnp.concatenate([flag[...]] * (columns // 128), axis=1) == 0


def cuts():
    return [pl.ds(at * CH, CH) for at in range(Q // CH)]


def combine_parts(flag, coefs, parts, mine, sent):
    even = is_even(flag)
    for cut in cuts():
        totals = spread_slices(coefs, parts, cut)
        for e, total in enumerate(totals):
            mine[e, :, cut] = total
        for z in range(ZD):
            sent[z, :, cut] = totals[4 + z].astype(BF16)
            sent[ZD + z, :, cut] = jnp.where(even, totals[8 + z], totals[z]).astype(BF16)


def open_kernel(flag, c0, c1, c2, c3, mine, sent, coefs):
    parts = (c0, c1, c2, c3)
    for r in range(ANG):
        for i in range(PAIR):
            value = parts[r][i, :, Q:].astype(F32)
            total = value[:, 0:1] + value[:, 1:2] + value[:, 2:3]
            coefs[r, i] = jnp.broadcast_to(total, (L, 128))
    combine_parts(flag, coefs, parts, mine, sent)


def combine_kernel(flag, coefs, c0, c1, c2, c3, mine, sent):
    combine_parts(flag, coefs, (c0, c1, c2, c3), mine, sent)


def edge_kernel(flag, mine, other, sent):
    even = is_even(flag, Q)
    for z in range(ZD):
        sent[z] = (mine[4 + z] + other[ZD + z].astype(F32)).astype(BF16)
        sent[ZD + z] = jnp.where(even, mine[z], mine[8 + z]).astype(BF16)


def pieces_body(flag, coefs, mine, other, outer, inner, g_out, outs, kept, note):
    even = is_even(flag)
    for cut in cuts():
        def get(ref, z):
            return ref[z, :, cut].astype(F32)

        cells = [None] * 12
        for z in range(ZD):
            beyond = get(outer, z)
            beside = get(other, z) + get(inner, 4 + z)
            cells[z] = mine[z, :, cut] + jnp.where(even, beyond, beside)
            cells[4 + z] = mine[4 + z, :, cut] + get(other, 4 + z) + get(outer, 4 + z)
            cells[8 + z] = mine[8 + z, :, cut] + jnp.where(even, beside, beyond)
            g_out[z, :, cut] = cells[4 + z]
            kept = note(kept, z, cut, cells[4 + z])
        for r in range(ANG):
            for i in range(PAIR):
                total = None
                for e in range(12):
                    term = coefs[r, i, e:e + 1, :] * cells[e]
                    total = term if total is None else total + term
                outs[r][i, :, cut] = total.astype(outs[r].dtype)
    return kept


def pieces_first(flag, coefs, mine, other, outer, inner, g_out, h0, h1, h2, h3, dots):
    def note(kept, z, cut, value):
        return kept + fold(value * value)

    dots[...] = pieces_body(
        flag, coefs, mine, other, outer, inner, g_out, (h0, h1, h2, h3), jnp.zeros((8, 128), F32), note
    )


def pieces_second(flag, coefs, g0, mine, other, outer, inner, g_out, h0, h1, h2, h3, dots):
    def note(kept, z, cut, value):
        return kept[0] + fold(value * g0[z, :, cut]), kept[1] + fold(value * value)

    dots[:8], dots[8:] = pieces_body(
        flag, coefs, mine, other, outer, inner, g_out, (h0, h1, h2, h3), (jnp.zeros((8, 128), F32),) * 2, note
    )


def last_kernel(flag, coefs, c0, c1, c2, c3, own, inner, outer):
    even = is_even(flag)
    for cut in cuts():
        totals = spread_slices(coefs, (c0, c1, c2, c3), cut)
        for z in range(ZD):
            own[z, :, cut] = totals[4 + z]
            inner[z, :, cut] = jnp.where(even, totals[8 + z], totals[z]).astype(BF16)
            outer[z, :, cut] = jnp.where(even, totals[z], totals[8 + z])


def steps(sums_ref):
    parts = [sums_ref[at] for at in range(16)]
    for at in range(16, sums_ref.shape[0]):
        parts[at % 16] = parts[at % 16] + sums_ref[at]
    while len(parts) > 1:
        parts = [low + high for low, high in zip(parts[::2], parts[1::2])]
    total = parts[0]
    lane = lax.broadcasted_iota(jnp.int32, (1, 128), 1)
    gamma0, curve0, inner, norm, cross, own = [
        jnp.sum(jnp.where(lane == at, total, 0.0)) for at in range(6)
    ]
    step0 = gamma0 / curve0
    gamma1 = gamma0 - 2.0 * step0 * inner + step0 * step0 * norm
    ratio = gamma1 / gamma0
    curve1 = (1.0 + ratio) * (1.0 + ratio) * curve0 - 2.0 * (1.0 + ratio) * step0 * cross + step0 * step0 * own
    step1 = gamma1 / curve1
    return step0 + step1 * (1.0 + ratio), step0 * step1


def volume_kernel(sums, g0, z0, out):
    one, two = steps(sums)
    for z in range(ZD):
        out[z] = (one * g0[z] - two * z0[z]).astype(BF16)


def gradient_kernel(sums, t1, inner, outer, g0, z0, out):
    one, two = steps(sums)
    for z in range(ZD):
        last = t1[z] + inner[z].astype(F32) + outer[z]
        out[z] = (g0[z] - one * z0[z] + two * last).astype(BF16)


def residual_kernel(sums, p, q0, w0, out):
    one, two = steps(sums)
    for a in range(PAIR):
        out[a, 0] = p[a, 0] - one * q0[a] + two * w0[a]


def place_kernel(me_ref, s0, s1, s2, s3, out):
    def place(at, share):
        out[:, :, at] = share[...].astype(F32)

    gather_shares(me_ref[0], (s0, s1, s2, s3), place)


def along_ang(value, other):
    return lax.ppermute(value, "ang", [(i, i ^ other) for i in range(ANG)])


def on_chip(value):
    return lax.ppermute(value, "slab", [(i, i ^ 1) for i in range(lax.axis_size("slab"))])


def across(value):
    count = lax.axis_size("slab")
    return lax.ppermute(
        value, "slab", [pair for i in range(1, count - 1, 2) for pair in ((i, i + 1), (i + 1, i))]
    )


def exchange(shares):
    return (shares[0],) + tuple(along_ang(shares[i], ORDER[i]) for i in range(1, ANG))


def per_device(projections, weights, columns, row_weights, reach):
    me = lax.axis_index("ang").astype(jnp.int32).reshape(1)
    parity = (lax.axis_index("slab").astype(jnp.int32) & 1).reshape(1)
    row = sds((PAIR * ZD, 128), F32)
    inner, own, outer, flag, cols, p = call(
        open_inputs, [row] * 3 + [sds((L, 128), jnp.int32), sds((3, PAIR, UB), jnp.int32), sds(projections.shape, F32)], [SMEM] + [HBM] * 4,
        [pltpu.SMEM(row_weights.shape, F32), pltpu.SMEM(reach.shape, jnp.int32), pltpu.SemaphoreType.DMA((4,))],
        limit=53,
    )(parity, row_weights, reach, columns.transpose(2, 0, 1), projections)
    outer = across(outer)
    edges = (flag, own, on_chip(inner), outer)

    def share(dtype, more=0):
        return sds((PAIR, L, Q + more), dtype)

    full = sds((PAIR, L, X), F32)
    part = sds((ZD, L, Q), F32)
    part_b = sds((ZD, L, Q), BF16)
    acc = pltpu.VMEM((PAIR, L, X), F32)
    macs = 2 * PAIR * L * UB * 384 * 128
    sent = [sds((3 * ZD, L, Q), F32), sds((2 * ZD, L, Q), BF16)]

    def halo(mine, sent):
        other = on_chip(sent)
        (edge,) = call(edge_kernel, [sds((2 * ZD, L, Q), BF16)], [VMEM] * 3)(flag, mine, other)
        outer = across(edge)
        return mine, other, outer, on_chip(outer)

    *shares, w = call(
        back_kernel, [share(BF16)] * 4 + [sds((PAIR, UB, 384, 128), BF16)],
        [SMEM] * 2 + [VMEM, HBM], [acc, pltpu.SemaphoreType.DMA((PAIR, UB // CHUNK))],
        flops=2 * macs, nbytes=7_000_000, limit=46,
    )(me, cols, p, weights.reshape(PAIR, UB, 384, 128))
    shares = call(stencil_kernel, [share(BF16, COEF)] * 4, [VMEM] * 8)(*edges, *shares)
    *spread, coefs = call(
        open_kernel, sent + [sds((ANG, PAIR, L, 128), F32)], [VMEM] * 5, flops=10_000_000
    )(flag, *exchange(shares))
    g0, *shares, gamma = call(
        pieces_first, [part] + [share(BF16)] * 4 + [sds((8, 128), F32)], [VMEM] * 6, flops=10_000_000
    )(flag, coefs, *halo(*spread))

    *shares, q0, curve = call(
        first_kernel, [share(MID)] * 4 + [full, sds((8, 128), F32)],
        [SMEM] * 2 + [VMEM] * 5, [pltpu.VMEM((PAIR, L, X), BF16), acc],
        flops=3 * macs, nbytes=7_000_000,
    )(me, cols, *exchange(shares), w)
    spread = call(combine_kernel, sent, [VMEM] * 6, flops=10_000_000)(flag, coefs, *exchange(shares))
    z0, *shares, inner = call(
        pieces_second, [part] + [share(BF16)] * 4 + [sds((16, 128), F32)], [VMEM] * 7, flops=10_000_000
    )(flag, coefs, g0, *halo(*spread))

    *shares, w0, sums = call(
        second_kernel, [share(F32)] * 4 + [full, sds((lax.axis_size("slab") * ANG, 1, 128), F32)],
        [SMEM] * 2 + [VMEM] * 9, [pltpu.VMEM((PAIR, L, X), BF16), acc],
        flops=4 * macs, nbytes=9_000_000,
    )(me, cols, *exchange(shares), q0, gamma, curve, inner, w)
    shares = exchange(shares)
    sums = lax.all_to_all(sums, ("slab", "ang"), 0, 0, tiled=True)
    own, inner, outer = call(last_kernel, [part, part_b, part], [VMEM] * 6, flops=10_000_000)(flag, coefs, *shares)
    outer = across(outer)
    inner = on_chip(inner)
    (volume,) = call(volume_kernel, [part_b], [VMEM] * 3)(sums, g0, z0)
    (residual,) = call(residual_kernel, [sds(projections.shape, F32)], [VMEM] * 4)(sums, projections, q0, w0)
    volume = exchange((volume,) * 4)
    (gradient,) = call(gradient_kernel, [part_b], [VMEM] * 6)(sums, own, inner, outer, g0, z0)
    whole = [sds((ZD, L, X), F32)]
    (volume,) = call(place_kernel, whole, [SMEM] + [VMEM] * 4)(me, *volume)
    (gradient,) = call(place_kernel, whole, [SMEM] + [VMEM] * 4)(me, *exchange((gradient,) * 4))
    return volume, residual, gradient


def solution(mesh):
    in_specs = (
        P("ang", "slab", None, None),
        P("ang", None, None, None, None),
        P("ang", None, None),
        P("ang", "slab", None, None, None),
        P("ang", "slab", None),
    )
    out_specs = (P("slab", None, None), P("ang", "slab", None, None), P("slab", None, None))
    return jax.shard_map(
        per_device, mesh=mesh, in_specs=in_specs, out_specs=out_specs, check_vma=False
    )
```
